256 devices in a mesh: ctx: 16 (over z, core), node: 4 (over y), dev: 4 (over x).
Axes of the slice: x: 4, y: 4, z: 8, core: 2. Of those that a mesh axis runs over, the one named last changes fastest.
Arguments:
- queries: bfloat16 [32, 128, 576], P('node'), may hold values from -6 to 6
- latent_cache: bfloat16 [32, 16384, 576], P('node', ('ctx', 'dev')), may hold values from -256 to 256
- block_ids: int32 [32, 32], P('node'), may hold values from 0 to 255, as said below
- value_lift_weight: bfloat16 [128, 512, 128], P(('ctx', 'dev')), may hold values from -0.25 to 0.25
- out_weight: bfloat16 [16384, 7168], P(('ctx', 'dev')), may hold values from -0.046875 to 0.046875
- residual: bfloat16 [32, 7168], P('node'), may hold values from -1.5 to 1.5
- norm_gain: bfloat16 [7168], replicated, may hold values from 0.099609375 to 1.8984375
- expert_ids: int32 [32, 8], replicated, may hold values from 0 to 15, all different within a row; in each aligned block of 8 rows (0 to 7, 8 to 15, ...) at most 6 rows name the same one
- expert_weights: float32 [32, 8], replicated, may hold values from 0.05 to 0.6
- gate_weight: bfloat16 [16, 7168, 2048], P(('node', 'dev'), None, 'ctx'), may hold values from -0.0625 to 0.0625
- up_weight: bfloat16 [16, 7168, 2048], P(('node', 'dev'), None, 'ctx'), may hold values from -0.0625 to 0.0625
- down_weight: bfloat16 [16, 2048, 7168], P(('node', 'dev'), 'ctx'), may hold values from -0.125 to 0.125
Outputs:
- layer_out: bfloat16 [32, 7168], P('node', ('ctx', 'dev'))
The draws below stay inside these ranges and needn't reach their ends.
Inputs may be any that keep to these rules, and one draw needn't show every extreme that they name: `block_ids`: each row names 32 different blocks; at most 2 of a row's blocks lie in one part of 4 blocks, and exactly 2 in some part of every row. `expert_ids`: in each aligned block of 8 rows no expert is named by more than 6 rows.
All inputs are finite; a program needn't handle non-finite values.
Results may differ from the reference program's by a relative error of at most 0.015.
Values may be sent and summed in bfloat16 or wider, within the bound.
A program may use at most 320 MiB of HBM per device.

```python
import math
import jax
import jax.numpy as jnp
import numpy as np
from jax import lax

D = 7168
HEAD_COUNT = 128
LATENT_WIDTH = 512
ROTARY_WIDTH = 64
VALUE_WIDTH = 128
FF = 2048
TOPK = 8
PICKED_BLOCKS = 32
BLOCK_POSITIONS = 64
ROWS_NODE = 8
DECODE_ROWS = 32
CACHE_LENGTH = 16384
BLK_DEV = 4
MOST_BLK = 2
EXPERTS = 16
CAP = 6
N_CTX = 16
N_DEV = 4


def chosen_blocks(key):
    key = jax.random.fold_in(key, 101)
    part_count = N_CTX * N_DEV

    def one_row(row_key):
        key_hot, key_order, key_perm, key_shuffle = jax.random.split(row_key, 4)
        hot = jax.random.randint(key_hot, (), 0, part_count)
        order = jax.random.permutation(key_order, (part_count - 1) * MOST_BLK)[:PICKED_BLOCKS - MOST_BLK]
        other = order // MOST_BLK
        place = order % MOST_BLK
        other = other + (other >= hot).astype(jnp.int32)
        within = jax.vmap(lambda part_key: jax.random.permutation(part_key, BLK_DEV))(jax.random.split(key_perm, part_count))
        hot_blocks = hot * BLK_DEV + within[hot, :MOST_BLK]
        other_blocks = other * BLK_DEV + within[other, place]
        joined = jnp.concatenate([hot_blocks, other_blocks]).astype(jnp.int32)
        return jax.random.permutation(key_shuffle, joined)
    return jax.vmap(one_row)(jax.random.split(key, DECODE_ROWS)).astype(jnp.int32)


def query_values(key):
    key = jax.random.fold_in(key, 202)
    return jax.random.truncated_normal(key, -6.0, 6.0, (DECODE_ROWS, HEAD_COUNT, LATENT_WIDTH + ROTARY_WIDTH), jnp.float32)


def draw_block_ids(key, part):
    return chosen_blocks(key)


def draw_queries(key, part):
    return query_values(key).astype(jnp.bfloat16)


def draw_latent_cache(key, part):
    key = jax.random.fold_in(key, 3)
    cache_table = 0.6 * jax.random.truncated_normal(key, -6.0, 6.0, (DECODE_ROWS, CACHE_LENGTH, LATENT_WIDTH + ROTARY_WIDTH), jnp.float32)
    return cache_table.astype(jnp.bfloat16)


def block_levels(stream_key, extent, shards, low, largest):
    level = 1.0
    for position, shards_of in shards:
        steps = jax.random.uniform(jax.random.fold_in(jax.random.fold_in(stream_key, 6), position), (shards_of,), jnp.float32, low / len(shards), largest / len(shards))
        level = level * jnp.repeat(jnp.exp(steps), extent[position] // shards_of).reshape((-1,) + (1,) * (len(extent) - 1 - position))
    return level


def routed_block(key, own, number, rows, count, top, limit, slope):
    ranking = jax.random.permutation(key, count)
    crowded, usual = load_shares(count, rows * top, limit, slope, True), load_shares(count, rows * top, limit, slope, False)
    places = jnp.arange(count)

    def named(tallies, offset_by):
        used = int((tallies > 0).sum())
        fixed = max(1, used // 4)
        passed = fixed + (places - fixed + offset_by * (used - fixed)) % max(1, count - fixed)
        return jnp.zeros((count,), jnp.int32).at[ranking[jnp.where(places < fixed, places, passed)]].set(jnp.asarray(tallies, jnp.int32))

    tallies = jnp.where(number % 4 == 0, named(crowded, number // 4), named(usual, number - number // 4 - 1))
    mixed = jax.random.permutation(jax.random.fold_in(own, 3), count)
    giver, taker = mixed[0:count // 2 * 2:2], mixed[1:count // 2 * 2:2]
    slack = jnp.minimum(tallies[giver] - 1, limit - tallies[taker]) // 2
    slack = jnp.where((giver == ranking[0]) | (taker == ranking[0]) | (tallies[taker] == 0), 0, jnp.maximum(slack, 0))
    passed = jax.random.randint(jax.random.fold_in(own, 4), (count // 2,), 0, 1 << 20) % (slack + 1)
    tallies = tallies.at[giver].add(-passed).at[taker].add(passed)
    members = jnp.searchsorted(jnp.cumsum(tallies), jnp.arange(rows * top), side="right").astype(jnp.int32)
    table = members.reshape(top, rows).T
    table = table[jax.random.permutation(jax.random.fold_in(own, 1), rows)]
    offset_by = jax.random.randint(jax.random.fold_in(own, 2), (rows, 1), 0, top)
    return jnp.take_along_axis(table, (jnp.arange(top)[None, :] + offset_by) % top, axis=1)


def load_shares(number_of, total, limit, lean, full):
    weights = [(1 << 20) // math.isqrt(rank ** lean) + 1 for rank in range(1, number_of + 1)]
    largest = limit if full else min(limit, max(-(-total // number_of), total * weights[0] // sum(weights)))
    least = 1 if total - largest >= number_of - 1 else 0
    holding, spare = [largest] + [least] * (number_of - 1), total - largest - least * (number_of - 1)
    while spare > 0:
        candidates = [i for i in range(1, number_of) if holding[i] < largest] or [i for i in range(1, number_of) if holding[i] < limit]
        whole, remaining = sum([weights[i] for i in candidates]), spare
        for i in candidates:
            more = min(limit - holding[i], max(1, remaining * weights[i] // whole), spare)
            holding[i] = holding[i] + more
            spare = spare - more
    return np.array(holding)


def centred(key, shape, scale, bound, cuts=(), kind=jnp.bfloat16):
    entries = jax.random.normal(key, shape, jnp.float32) * scale
    if len(cuts) > 0:
        entries = block_levels(key, shape, cuts, -0.22, 0.18) * entries
    return jnp.clip(entries, min=-bound, max=bound).astype(kind)


def setup_inputs(seed: int = 0) -> dict:
    keys = jax.random.split(jax.random.key(seed), 13)
    queries = draw_queries(jax.random.fold_in(keys[12], 71), 0)
    latent_cache = draw_latent_cache(jax.random.fold_in(keys[12], 71), 0)
    block_ids = draw_block_ids(jax.random.fold_in(keys[12], 71), 0)
    value_lift_weight = centred(keys[3], (HEAD_COUNT, LATENT_WIDTH, VALUE_WIDTH), LATENT_WIDTH ** -0.5, 0.25, ((0, 64),))
    out_weight = centred(keys[4], (HEAD_COUNT * VALUE_WIDTH, D), (HEAD_COUNT * VALUE_WIDTH) ** -0.5, 0.046875, ((0, 64),))
    residual = centred(keys[5], (DECODE_ROWS, D), 0.25, 1.5, ((0, 4),))
    norm_gain = jnp.clip(1.0 + 0.18 * jax.random.normal(keys[6], (D,), jnp.float32), 0.099609375, 1.8984375).astype(jnp.bfloat16)
    expert_ids_keys = jax.random.split(jax.random.fold_in(keys[7], 1), DECODE_ROWS // ROWS_NODE)
    expert_ids_turns = jax.random.permutation(jax.random.fold_in(keys[7], 3), DECODE_ROWS // ROWS_NODE)
    expert_ids = jax.vmap(lambda own, number: routed_block(jax.random.fold_in(keys[7], 2), own, number, ROWS_NODE, EXPERTS, TOPK, CAP, 2))(expert_ids_keys, expert_ids_turns).reshape((DECODE_ROWS, TOPK))
    expert_weights = jnp.clip(jax.random.uniform(keys[8], (DECODE_ROWS, TOPK), jnp.float32, 0.05, 0.6), 0.05, 0.6)
    gate_weight = centred(keys[9], (EXPERTS, D, FF), D ** -0.5, 0.0625, ((0, 16), (2, 16)))
    up_weight = centred(keys[10], (EXPERTS, D, FF), D ** -0.5, 0.0625, ((0, 16), (2, 16)))
    down_weight = centred(keys[11], (EXPERTS, FF, D), FF ** -0.5, 0.125, ((0, 16), (1, 16)))
    return dict(queries=queries, latent_cache=latent_cache, block_ids=block_ids, value_lift_weight=value_lift_weight, out_weight=out_weight, residual=residual, norm_gain=norm_gain, expert_ids=expert_ids, expert_weights=expert_weights, gate_weight=gate_weight, up_weight=up_weight, down_weight=down_weight)


score_scale = 192.0 ** (-0.5) * (0.1 * math.log(40.0) + 1.0) ** 2
norm_eps = 1e-06

def attend_row(operands):
    query_rows, cache_rows, blocks = operands
    offsets = jnp.arange(BLOCK_POSITIONS, dtype=jnp.int32)
    positions = (blocks[:, None] * BLOCK_POSITIONS + offsets[None, :]).reshape(-1).astype(jnp.int32)
    key_rows = jnp.take(cache_rows, positions, axis=0)
    scores = jnp.dot(query_rows, key_rows.T, preferred_element_type=jnp.float32) * score_scale
    scores = scores.reshape(HEAD_COUNT, PICKED_BLOCKS, BLOCK_POSITIONS)
    block_max = lax.optimization_barrier(jnp.max(scores, axis=2))
    owner = blocks // BLK_DEV
    same_part = owner[:, None] == owner[None, :]
    part_max = lax.optimization_barrier(jnp.max(jnp.where(same_part[None, :, :], block_max[:, None, :], -jnp.inf), axis=2))
    probabilities = jnp.exp(scores - part_max[:, :, None]).astype(jnp.bfloat16)
    peak = lax.optimization_barrier(jnp.max(block_max, axis=1))
    factor = jnp.exp(part_max - peak[:, None])
    value_rows = key_rows[:, :LATENT_WIDTH].reshape(PICKED_BLOCKS, BLOCK_POSITIONS, LATENT_WIDTH)
    block_num = jnp.einsum('hst,stc->hsc', probabilities.astype(jnp.float32), value_rows.astype(jnp.float32))
    numer = jnp.einsum('hs,hsc->hc', factor, block_num)
    total = lax.optimization_barrier(jnp.sum(factor * lax.optimization_barrier(jnp.sum(probabilities.astype(jnp.float32), axis=2)), axis=1))
    return (numer / total[:, None]).astype(jnp.bfloat16)

def reference(queries, latent_cache, block_ids, value_lift_weight, out_weight, residual, norm_gain, expert_ids, expert_weights, gate_weight, up_weight, down_weight):
    latent_out = lax.map(attend_row, (queries, latent_cache, block_ids))
    head_values = jnp.einsum('rhc,hcv->rhv', latent_out.astype(jnp.float32), value_lift_weight.astype(jnp.float32)).astype(jnp.bfloat16)
    attention = jnp.dot(head_values.reshape(DECODE_ROWS, HEAD_COUNT * VALUE_WIDTH), out_weight, preferred_element_type=jnp.float32)
    state = (residual.astype(jnp.float32) + attention).astype(jnp.bfloat16)
    state_wide = state.astype(jnp.float32)
    mean_square = lax.optimization_barrier(jnp.mean(state_wide * state_wide, axis=1, keepdims=True))
    normed = (state_wide * lax.rsqrt(mean_square + norm_eps) * norm_gain.astype(jnp.float32)).astype(jnp.bfloat16)

    def expert_step(mixture, operands):
        gate_part, up_part, down_part, expert = operands
        coef = lax.optimization_barrier(jnp.sum(jnp.where(expert_ids == expert, expert_weights, jnp.float32(0.0)), axis=1))
        gate = jnp.dot(normed, gate_part, preferred_element_type=jnp.float32)
        upper = jnp.dot(normed, up_part, preferred_element_type=jnp.float32)
        hidden = (jax.nn.silu(gate) * upper).astype(jnp.bfloat16)
        result = jnp.dot(hidden, down_part, preferred_element_type=jnp.float32)
        return (mixture + coef[:, None] * result, None)
    start = jnp.zeros((DECODE_ROWS, D), jnp.float32)
    experts_seq = jnp.arange(EXPERTS, dtype=jnp.int32)
    mixture, unused = lax.scan(expert_step, start, (gate_weight, up_weight, down_weight, experts_seq))
    return (state.astype(jnp.float32) + mixture).astype(jnp.bfloat16)
```

```python
import math

import jax
import jax.numpy as jnp
from jax import lax
from jax.experimental import pallas as pl
from jax.experimental.pallas import tpu as pltpu
from jax.sharding import PartitionSpec as P

MESH = pl.DeviceIdType.MESH
F32, BF16 = jnp.float32, jnp.bfloat16
score_scale = 192.0 ** (-0.5) * (0.1 * math.log(40.0) + 1.0) ** 2
floor_score = -1e30
norm_eps = 1e-06

PAIRS = (
    ("a1", 4), ("s1", 8), ("s2", 8), ("a2", 4), ("a3", 8), ("a4", 8), ("b1", 8),
    ("b2", 8), ("c1", 16), ("c2", 16), ("d1", 8), ("d2", 4), ("d3", 8), ("d4", 4),
)
BUFFERS = (
    ("qv", (8, 576, 128), BF16), ("cv", (8, 576, 256), BF16), ("liftv", (2, 512, 128), BF16),
    ("wov", (256, 7168), BF16), ("wguv", (7168, 256), BF16), ("wdv", (128, 7168), BF16),
    ("keep", (8, 256), F32), ("probs", (8, 128, 256), BF16), ("colstat", (128, 128), F32),
    ("st1", (8, 16, 128), F32), ("st2", (8, 16, 128), F32), ("fcol", (128, 128), F32),
    ("a1own", (4, 128, 512), F32), ("a1snd", (4, 128, 512), BF16), ("a1rcv", (4, 128, 512), BF16),
    ("a2own", (8, 16, 512), F32), ("a2snd", (4, 8, 16, 512), BF16), ("a2rcv", (4, 8, 16, 512), BF16),
    ("a3snd", (8, 16, 512), BF16), ("a3rcv", (8, 16, 512), BF16), ("lat", (8, 16, 512), BF16),
    ("b1snd", (8, 16, 512), BF16), ("b1rcv", (8, 16, 512), BF16), ("part", (8, 16, 512), BF16),
    ("state", (32, 16, 512), BF16), ("normed", (8, 64, 512), BF16), ("gain", (8, 16, 512), F32),
    ("d1own", (8, 32, 512), F32), ("d1snd", (8, 32, 512), BF16), ("d1rcv", (8, 32, 512), BF16),
    ("d2snd", (4, 4, 16, 512), BF16), ("d2rcv", (4, 4, 16, 512), BF16), ("fin", (8, 8, 512), F32),
    ("d3snd", (8, 16, 256), BF16), ("d3rcv", (8, 16, 256), BF16),
    ("d4snd", (16, 256), BF16), ("d4rcv", (4, 16, 256), BF16),
)


class Names:
    pass


def dot(a, b, dims=((1,), (0,))):
    return lax.dot_general(a, b, (dims, ((), ())), preferred_element_type=F32)


def iota(shape, dim):
    return lax.broadcasted_iota(jnp.int32, shape, dim)


def kernel(ids_ref, gain_ref, eid_ref, ew_ref, res_ref, q_hbm, c_hbm, lift_hbm, wo_hbm, wg_hbm, wu_hbm, wd_hbm,
           out_ref, *scratch):
    v = Names()
    for (name, _, _), ref in zip(BUFFERS, scratch):
        setattr(v, name, ref)
    rest = scratch[len(BUFFERS):]
    local = rest[0]
    sems = {name: (rest[1 + 2 * i], rest[2 + 2 * i]) for i, (name, _) in enumerate(PAIRS)}

    ctx, node, dev = lax.axis_index("ctx"), lax.axis_index("node"), lax.axis_index("dev")
    z, core = lax.div(ctx, 2), lax.rem(ctx, 2)
    other = 1 - core
    g = core * 4 + dev
    shard = ctx * 4 + dev
    expert = node * 4 + dev

    def turn(a, k, n):
        return lax.rem(a + k, n)

    def at(ctx=ctx, node=node, dev=dev):
        return {"ctx": ctx, "node": node, "dev": dev}

    def at_core():
        return at(ctx=z * 2 + other)

    def at_z(k):
        return at(ctx=turn(z, k, 8) * 2 + core)

    def at_g(k):
        there = turn(g, k, 8)
        return at(ctx=z * 2 + lax.div(there, 4), dev=lax.rem(there, 4))

    def remote(name, slot, src, dst, where):
        send, recv = sems[name]
        return pltpu.make_async_remote_copy(
            src_ref=src, dst_ref=dst, send_sem=send.at[slot], recv_sem=recv.at[slot],
            device_id=where, device_id_type=MESH,
        )

    sent = []

    def push(*args):
        copy = remote(*args)
        copy.start()
        sent.append(copy)
        return copy

    def row_at(i):
        return jnp.where(i < 4, other, core) * 4 + lax.rem(dev + 1 + i, 4)

    def fetch_q(i):
        r = row_at(i)
        return pltpu.make_async_copy(q_hbm.at[r], v.qv.at[r], local.at[i])

    def fetch_c(i):
        r = row_at(i)
        return pltpu.make_async_copy(c_hbm.at[r], v.cv.at[r], local.at[8 + i])

    for i in range(8):
        fetch_q(i).start()
        fetch_c(i).start()
    fetch_lift = pltpu.make_async_copy(lift_hbm, v.liftv, local.at[16])
    fetch_wo = pltpu.make_async_copy(wo_hbm, v.wov, local.at[17])
    fetch_wg = pltpu.make_async_copy(wg_hbm.at[0], v.wguv.at[:, pl.ds(0, 128)], local.at[18])
    fetch_wu = pltpu.make_async_copy(wu_hbm.at[0], v.wguv.at[:, pl.ds(128, 128)], local.at[19])
    fetch_wd = pltpu.make_async_copy(wd_hbm.at[0], v.wdv, local.at[20])
    for copy in (fetch_lift, fetch_wo, fetch_wg, fetch_wu, fetch_wd):
        copy.start()

    barrier = pltpu.get_barrier_semaphore()
    partners = [at_g(k) for k in range(1, 8)] + [at_z(k) for k in range(1, 8)]
    partners += [at(node=turn(node, i, 4), dev=turn(dev, j, 4)) for i in range(1, 4) for j in range(4)]
    for where in partners:
        pl.semaphore_signal(barrier, inc=1, device_id=where, device_id_type=MESH)

    ids = ids_ref[...]
    block = lax.div(iota((8, 256), 1), 64)
    keep = jnp.zeros((8, 256), F32)
    for b in range(4):
        hit = jnp.max(jnp.where(ids == shard * 4 + b, 1.0, 0.0), axis=1, keepdims=True)
        keep = jnp.where(block == b, hit, keep)
    v.keep[...] = keep
    v.colstat[...] = jnp.zeros((128, 128), F32)
    lanes = iota((128, 128), 1)

    @pl.loop(0, 8)
    def _(i):
        r = row_at(i)
        fetch_q(i).wait()
        fetch_c(i).wait()
        kept = v.keep[pl.ds(r, 1), :] > 0.5
        scores = dot(v.qv[r], v.cv[r], ((0,), (0,))) * score_scale
        scores = jnp.where(kept, scores, floor_score)
        top = jnp.max(scores, axis=1, keepdims=True)
        probs = jnp.where(kept, jnp.exp(scores - top), 0.0).astype(BF16)
        total = jnp.sum(probs.astype(F32), axis=1, keepdims=True)
        v.probs[r] = probs
        v.colstat[...] = jnp.where(lanes == r, top, jnp.where(lanes == r + 8, total, v.colstat[...]))

    v.st1[g] = v.colstat[...].T[:16, :]
    pl.semaphore_wait(barrier, len(partners))
    s1 = [push("s1", k, v.st1.at[g], v.st1.at[g], at_g(k)) for k in range(1, 8)]

    def weighted(r):
        return dot(v.probs[r], v.cv[r, :512, :], ((1,), (1,)))

    def send_a1(j):
        xj = lax.rem(dev + 1 + j, 4)
        return remote("a1", j, v.a1snd.at[xj], v.a1rcv.at[xj], at_core())

    @pl.loop(0, 4)
    def _(j):
        xj = lax.rem(dev + 1 + j, 4)
        v.a1snd[xj] = weighted(other * 4 + xj).astype(BF16)
        send_a1(j).start()

    def joined(ref):
        peak = ref[0, :8, :]
        for i in range(1, 8):
            peak = jnp.maximum(peak, ref[i, :8, :])
        total = jnp.zeros((8, 128), F32)
        for i in range(8):
            total += ref[i, 8:, :] * jnp.exp(ref[i, :8, :] - peak)
        return peak, total

    for copy in s1:
        copy.wait_recv()
    peak, total = joined(v.st1)
    v.st2[z, :8, :] = peak
    v.st2[z, 8:, :] = total
    s2 = [push("s2", k, v.st2.at[z], v.st2.at[z], at_z(k)) for k in range(1, 8)]

    @pl.loop(0, 4)
    def _(j):
        xj = lax.rem(dev + 1 + j, 4)
        v.a1own[xj] = weighted(core * 4 + xj)

    for copy in s2:
        copy.wait_recv()
    peak, total = joined(v.st2)
    here = jnp.exp(v.st1[g, :8, :] - peak) / total
    there = jnp.exp(v.st1[other * 4 + dev, :8, :] - peak) / total
    v.fcol[...] = jnp.concatenate([here, there, jnp.zeros((112, 128), F32)], axis=0).T

    a2 = []
    for j in range(4):
        xj = lax.rem(dev + 1 + j, 4)
        r = core * 4 + xj
        f_here = jnp.sum(jnp.where(lanes == r, v.fcol[...], 0.0), axis=1, keepdims=True)
        f_there = jnp.sum(jnp.where(lanes == r + 8, v.fcol[...], 0.0), axis=1, keepdims=True)
        send_a1(j).wait_recv()
        both = f_here * v.a1own[xj] + f_there * v.a1rcv[xj].astype(F32)
        both = both.reshape(8, 16, 512)
        if j < 3:
            v.a2snd[xj] = both.astype(BF16)
            a2.append(push("a2", j, v.a2snd.at[xj], v.a2rcv.at[j], at(dev=xj)))
        else:
            v.a2own[...] = both
    for copy in a2:
        copy.wait_recv()

    def row_heads(zt):
        summed = v.a2own[zt]
        for j in range(3):
            summed += v.a2rcv[j, zt].astype(F32)
        return summed

    a3 = []
    for k in range(1, 8):
        zt = turn(z, k, 8)
        v.a3snd[zt] = row_heads(zt).astype(BF16)
        a3.append(push("a3", k, v.a3snd.at[zt], v.a3rcv.at[k], at_z(k)))
    summed = row_heads(z)
    for k, copy in enumerate(a3, 1):
        copy.wait_recv()
        summed += v.a3rcv[k].astype(F32)
    v.lat[g] = summed.astype(BF16)

    a4 = [push("a4", k, v.lat.at[g], v.lat.at[g], at_g(k)) for k in range(1, 8)]
    pick_row, pick_lane = iota((16, 128), 0), iota((16, 128), 1)
    pick = (lax.div(pick_lane, 16) == lax.rem(pick_row, 8)) & (
        lax.rem(pick_lane, 16) == core * 8 + dev * 2 + lax.div(pick_row, 8)
    )
    pick = jnp.where(pick, 1.0, 0.0).astype(BF16)
    for i in range(8):
        for t in range(4):
            row = i * 7 + t
            v.gain[i, :8, t * 128:t * 128 + 128] = jnp.broadcast_to(gain_ref[row:row + 1, :].astype(F32), (8, 128))
            v.gain[i, 8:, t * 128:t * 128 + 128] = jnp.broadcast_to(gain_ref[row + 3:row + 4, :].astype(F32), (8, 128))
    fetch_lift.wait()
    fetch_wo.wait()
    for copy in a4:
        copy.wait_recv()
    own_heads = dot(pick, v.lat[...].reshape(128, 512)).astype(BF16)
    values = jnp.concatenate([dot(own_heads, v.liftv[0])[:8], dot(own_heads, v.liftv[1])[8:]], axis=1).astype(BF16)

    def projected(i):
        upper = dot(values, v.wov[:, pl.ds(pl.multiple_of(i * 896, 128), 512)])
        lower = dot(values, v.wov[:, pl.ds(pl.multiple_of(i * 896 + 512, 128), 384)])
        return jnp.concatenate([upper, jnp.concatenate([upper[:, 384:], lower], axis=1)], axis=0)

    b1 = []
    for k in range(1, 8):
        gt = turn(g, k, 8)
        v.b1snd[gt] = projected(gt).astype(BF16)
        b1.append(push("b1", k, v.b1snd.at[gt], v.b1rcv.at[k], at_g(k)))
    summed = projected(g)
    for k, copy in enumerate(b1, 1):
        copy.wait_recv()
        summed += v.b1rcv[k].astype(F32)
    v.part[z] = summed.astype(BF16)
    b2 = [push("b2", k, v.part.at[z], v.part.at[z], at_z(k)) for k in range(1, 8)]
    residual = jnp.concatenate(
        [
            res_ref[:, pl.ds(pl.multiple_of(g * 896, 128), 512)].astype(F32),
            res_ref[:, pl.ds(pl.multiple_of(g * 896 + 384, 128), 512)].astype(F32),
        ],
        axis=0,
    )
    for copy in b2:
        copy.wait_recv()
    attention = v.part[0].astype(F32)
    for i in range(1, 8):
        attention += v.part[i].astype(F32)
    mine = node * 8 + g
    v.state[mine] = (residual + attention).astype(BF16)

    c1, c2 = [], []
    for i in range(4):
        for j in range(4):
            if i + j > 0:
                where = at(node=turn(node, i, 4), dev=turn(dev, j, 4))
                c1.append((i, j, push("c1", i * 4 + j, v.state.at[mine], v.state.at[mine], where)))
    c2.append(push("c2", 0, v.state.at[mine], v.state.at[mine], at_core()))
    for i, j, copy in c1:
        copy.wait_recv()
        came = turn(node, 4 - i, 4) * 8 + core * 4 + turn(dev, 4 - j, 4)
        c2.append(push("c2", i * 4 + j, v.state.at[came], v.state.at[came], at_core()))
    for copy in c2:
        copy.wait_recv()

    row16, lane512 = iota((16, 512), 0), iota((16, 512), 1)
    once = (row16 < 8) | (lane512 >= 128)

    @pl.loop(0, 4)
    def _(y):
        squares = jnp.zeros((16, 512), F32)
        for i in range(8):
            wide = v.state[y * 8 + i].astype(F32)
            squares += wide * wide
        squares = jnp.sum(jnp.where(once, squares, 0.0), axis=1, keepdims=True)
        scale = lax.rsqrt((squares[:8] + squares[8:]) / 7168.0 + norm_eps)
        scale = jnp.concatenate([scale, scale], axis=0)
        for i in range(8):
            wide = v.state[y * 8 + i].astype(F32)
            v.normed[i, pl.ds(pl.multiple_of(y * 16, 16), 16), :] = (wide * scale * v.gain[i]).astype(BF16)

    fetch_wg.wait()
    fetch_wu.wait()
    upper = jnp.zeros((64, 256), F32)
    lower = jnp.zeros((64, 256), F32)
    for i in range(8):
        upper += dot(v.normed[i], v.wguv[i * 896:i * 896 + 512, :])
        lower += dot(v.normed[i, :, 128:], v.wguv[i * 896 + 512:i * 896 + 896, :])
    both = jnp.concatenate([upper[y * 16:y * 16 + 8] + lower[y * 16 + 8:y * 16 + 16] for y in range(4)], axis=0)
    gate, up = both[:, :128], both[:, 128:]
    coef = jnp.sum(jnp.where(eid_ref[...] == expert, ew_ref[...], 0.0), axis=0, keepdims=True)
    coef = jnp.sum(jnp.where(iota((32, 32), 0) == iota((32, 32), 1), coef, 0.0), axis=1, keepdims=True)
    hidden = (gate / (1.0 + jnp.exp(-gate)) * up * coef).astype(BF16)

    fetch_wd.wait()

    def lifted(i, c):
        return dot(hidden, v.wdv[:, pl.ds(pl.multiple_of(i * 896 + c * 384, 128), 512)])

    d1 = []
    for i in range(8):
        v.d1snd[i] = lifted(i, other).astype(BF16)
        d1.append(push("d1", i, v.d1snd.at[i], v.d1rcv.at[i], at_core()))
    for i in range(8):
        v.d1own[i] = lifted(i, core)
    for i in range(8):
        d1[i].wait_recv()
        v.d1own[i] = v.d1own[i] + v.d1rcv[i].astype(F32)
    d2 = []
    for k in range(1, 4):
        yt = turn(node, k, 4)
        rows = pl.ds(pl.multiple_of(yt * 8, 8), 8)
        for i in range(4):
            pair = jnp.concatenate([v.d1own[2 * i, rows, :], v.d1own[2 * i + 1, rows, :]], axis=0)
            v.d2snd[yt, i] = pair.astype(BF16)
        d2.append(push("d2", k, v.d2snd.at[yt], v.d2rcv.at[k], at(node=yt)))
    for copy in d2:
        copy.wait_recv()
    rows = pl.ds(pl.multiple_of(node * 8, 8), 8)
    for i in range(4):
        pair = jnp.concatenate([v.d1own[2 * i, rows, :], v.d1own[2 * i + 1, rows, :]], axis=0)
        for k in range(1, 4):
            pair += v.d2rcv[k, i].astype(F32)
        v.fin[2 * i] = pair[:8]
        v.fin[2 * i + 1] = pair[8:]

    def folded(wide):
        return jnp.concatenate([wide[:, :256], wide[:, 256:]], axis=0)

    d3 = []
    for k in range(1, 8):
        zt = turn(z, k, 8)
        v.d3snd[zt] = folded(v.fin[zt]).astype(BF16)
        d3.append(push("d3", k, v.d3snd.at[zt], v.d3rcv.at[k], at_z(k)))
    mixture = folded(v.fin[z])
    for k, copy in enumerate(d3, 1):
        copy.wait_recv()
        mixture += v.d3rcv[k].astype(F32)
    v.d4snd[...] = mixture.astype(BF16)
    d4 = [push("d4", k, v.d4snd, v.d4rcv.at[k], at(dev=turn(dev, k, 4))) for k in range(1, 4)]
    own = v.state[node * 8 + z].astype(F32)
    own = jnp.where(core == 0, own[:8], own[8:])
    for k, copy in enumerate(d4, 1):
        copy.wait_recv()
        mixture += v.d4rcv[k].astype(F32)
    mixture = jnp.concatenate([mixture[:8], mixture[8:]], axis=1)
    layer = (own + mixture).astype(BF16)
    chosen = iota((512, 112), 0) == iota((512, 112), 1) + core * 64 + dev * 112
    out_ref[...] = dot(layer, jnp.where(chosen, 1.0, 0.0).astype(BF16)).astype(BF16)

    for j in range(4):
        send_a1(j).wait_send()
    for copy in sent:
        copy.wait_send()


def shards(queries, latent_cache, block_ids, value_lift_weight, out_weight, residual, norm_gain, expert_ids,
           expert_weights, gate_weight, up_weight, down_weight):
    vmem, anywhere = pl.BlockSpec(memory_space=pltpu.VMEM), pl.BlockSpec(memory_space=pl.ANY)
    scratch = [pltpu.VMEM(shape, dtype) for _, shape, dtype in BUFFERS]
    scratch.append(pltpu.SemaphoreType.DMA((21,)))
    for _, count in PAIRS:
        scratch += [pltpu.SemaphoreType.DMA((count,)), pltpu.SemaphoreType.DMA((count,))]
    return pl.pallas_call(
        kernel,
        out_shape=jax.ShapeDtypeStruct((8, 112), BF16),
        in_specs=[vmem] * 5 + [anywhere] * 7,
        out_specs=vmem,
        scratch_shapes=scratch,
        compiler_params=pltpu.CompilerParams(
            collective_id=0, has_side_effects=True, vmem_limit_bytes=56 * 1024 * 1024
        ),
        name="layer",
    )(
        block_ids, norm_gain.reshape(56, 128), expert_ids.T, expert_weights.T, residual,
        jnp.swapaxes(queries, 1, 2), jnp.swapaxes(latent_cache, 1, 2),
        value_lift_weight, out_weight, gate_weight, up_weight, down_weight,
    )


def solution(mesh):
    placed = (
        P("node", None, None),
        P("node", ("ctx", "dev"), None),
        P("node", None),
        P(("ctx", "dev"), None, None),
        P(("ctx", "dev"), None),
        P("node", None),
        P(),
        P(),
        P(),
        P(("node", "dev"), None, "ctx"),
        P(("node", "dev"), None, "ctx"),
        P(("node", "dev"), "ctx", None),
    )
    return jax.shard_map(
        shards, mesh=mesh, in_specs=placed, out_specs=P("node", ("ctx", "dev")), check_vma=False
    )
```

```python
import math

import jax
import jax.numpy as jnp
from jax import lax
from jax.experimental import pallas as pl
from jax.experimental.pallas import tpu as pltpu
from jax.sharding import PartitionSpec as P

MESH = pl.DeviceIdType.MESH
F32, BF16 = jnp.float32, jnp.bfloat16
score_scale = 192.0 ** (-0.5) * (0.1 * math.log(40.0) + 1.0) ** 2
floor_score = -1e30
norm_eps = 1e-06

PAIRS = (
    ("a1", 8), ("s1", 8), ("s2", 8), ("a2", 8), ("a3", 8), ("b1", 8),
    ("b2", 8), ("c1", 16), ("c2", 4), ("wd", 1), ("hid", 1), ("d2", 16), ("d3", 8),
)
BUFFERS = (
    ("qv", (8, 576, 128), BF16), ("cv", (8, 576, 256), BF16), ("liftv", (2, 512, 128), BF16),
    ("wov", (256, 7168), BF16), ("wguv", (7168, 256), BF16), ("wdv", (128, 7168), BF16),
    ("keep", (8, 256), F32), ("probs", (8, 128, 256), BF16),
    ("st1", (8, 16, 128), F32), ("st2", (8, 16, 128), F32), ("fcol", (128, 128), F32),
    ("a1own", (8, 64, 512), F32), ("a1snd", (8, 64, 512), BF16), ("a1rcv", (8, 64, 512), BF16),
    ("a2snd", (4, 8, 16, 512), BF16), ("a2rcv", (4, 8, 16, 512), BF16),
    ("a3snd", (8, 16, 512), BF16), ("a3rcv", (8, 16, 512), BF16),
    ("b1snd", (8, 16, 512), BF16), ("b1rcv", (8, 16, 512), BF16), ("part", (8, 16, 512), BF16),
    ("state", (32, 16, 512), BF16), ("normed", (4, 64, 512), BF16), ("gain", (8, 16, 512), F32),
    ("select", (4, 384, 256), BF16), ("laid", (2, 128, 4096), BF16), ("down", (256, 4096), BF16),
    ("hidden", (2, 32, 128), BF16), ("d2snd", (16, 4, 16, 128), BF16), ("d2rcv", (16, 4, 16, 128), BF16),
    ("d3snd", (8, 8, 128), F32), ("d3rcv", (8, 8, 128), F32),
)


class Names:
    pass


def dot(a, b, dims=((1,), (0,))):
    return lax.dot_general(a, b, (dims, ((), ())), preferred_element_type=F32)


def iota(shape, dim):
    return lax.broadcasted_iota(jnp.int32, shape, dim)


def kernel(ids_ref, gain_ref, eid_ref, ew_ref, res_ref, q_hbm, c_hbm, lift_hbm, wo_hbm, wg_hbm, wu_hbm, wd_hbm,
           out_ref, *scratch):
    v = Names()
    for (name, _, _), ref in zip(BUFFERS, scratch):
        setattr(v, name, ref)
    rest = scratch[len(BUFFERS):]
    local = rest[0]
    sems = {name: (rest[1 + 2 * i], rest[2 + 2 * i]) for i, (name, _) in enumerate(PAIRS)}

    ctx, node, dev = lax.axis_index("ctx"), lax.axis_index("node"), lax.axis_index("dev")
    z, core = lax.div(ctx, 2), lax.rem(ctx, 2)
    other = 1 - core
    g = core * 4 + dev
    shard = ctx * 4 + dev
    expert = node * 4 + dev

    def turn(a, k, n):
        return lax.rem(a + k, n)

    def at(ctx=ctx, node=node, dev=dev):
        return {"ctx": ctx, "node": node, "dev": dev}

    def at_core():
        return at(ctx=z * 2 + other)

    def at_z(k):
        return at(ctx=turn(z, k, 8) * 2 + core)

    def at_g(k):
        there = turn(g, k, 8)
        return at(ctx=z * 2 + lax.div(there, 4), dev=lax.rem(there, 4))

    def remote(name, slot, src, dst, where):
        send, recv = sems[name]
        return pltpu.make_async_remote_copy(
            src_ref=src, dst_ref=dst, send_sem=send.at[slot], recv_sem=recv.at[slot],
            device_id=where, device_id_type=MESH,
        )

    sent, fetches = [], []

    def push(*args):
        copy = remote(*args)
        copy.start()
        sent.append(copy)
        return copy

    far_z, far_g = (4, 3, 5, 2, 6, 1, 7), (2, 6, 1, 3, 5, 7, 4)

    def hops(i, j):
        return min(i, 4 - i) + min(j, 4 - j)

    far_xy = sorted(((i, j) for i in range(4) for j in range(4) if i + j), key=lambda step: -hops(*step))

    def fetch_q(r):
        return pltpu.make_async_copy(q_hbm.at[r], v.qv.at[r], local.at[r])

    def fetch_c(r):
        return pltpu.make_async_copy(c_hbm.at[r], v.cv.at[r], local.at[8 + r])

    for i in range(8):
        fetch_q(i).start()
        fetch_c(i).start()
    fetch_lift = pltpu.make_async_copy(lift_hbm, v.liftv, local.at[16])
    fetch_wo = pltpu.make_async_copy(wo_hbm, v.wov, local.at[17])
    fetch_wg = pltpu.make_async_copy(wg_hbm.at[0], v.wguv.at[:, pl.ds(0, 128)], local.at[18])
    fetch_wu = pltpu.make_async_copy(wu_hbm.at[0], v.wguv.at[:, pl.ds(128, 128)], local.at[19])
    fetch_wd = pltpu.make_async_copy(wd_hbm.at[0], v.wdv, local.at[20])
    for copy in (fetch_lift, fetch_wo, fetch_wg, fetch_wu, fetch_wd):
        copy.start()
        fetches.append(copy)

    def ready(*copies):
        for copy in copies:
            fetches[:] = [other_copy for other_copy in fetches if other_copy is not copy]
            copy.wait()

    barrier = pltpu.get_barrier_semaphore()
    partners = [(min(k, 8 - k), at_z(k)) for k in far_z]
    partners += [(2 if k in (2, 6) else k % 2, at_g(k)) for k in far_g]
    partners += [(hops(i, j), at(node=turn(node, i, 4), dev=turn(dev, j, 4))) for i in range(1, 4) for j in range(4)]
    for _, where in sorted(partners, key=lambda partner: -partner[0]):
        pl.semaphore_signal(barrier, inc=1, device_id=where, device_id_type=MESH)

    ids = ids_ref[...]
    block = lax.div(iota((8, 256), 1), 64)
    keep = jnp.zeros((8, 256), F32)
    for b in range(4):
        hit = jnp.max(jnp.where(ids == shard * 4 + b, 1.0, 0.0), axis=1, keepdims=True)
        keep = jnp.where(block == b, hit, keep)
    v.keep[...] = keep

    def one_hot(hit):
        return jnp.where(hit, 1.0, 0.0).astype(BF16)

    at_row, at_col = iota((128, 128), 0), iota((128, 128), 1)

    def part_of(number, low, size):
        return lax.rem(lax.div(number, low), size)

    by_owner = one_hot(
        at_col == part_of(at_row, 2, 8) * 16 + part_of(at_row, 64, 2) * 8 + part_of(at_row, 16, 4) * 2 + part_of(at_row, 1, 2)
    )
    stats = jnp.zeros((128, 128), F32)
    for r in range(8):
        fetch_q(r).wait()
        fetch_c(r).wait()
        kept = v.keep[r:r + 1, :] > 0.5
        heads = dot(by_owner, v.qv[r], ((1,), (1,))).astype(BF16)
        scores = dot(heads, v.cv[r]) * score_scale
        scores = jnp.where(kept, scores, floor_score)
        top = jnp.max(scores, axis=1, keepdims=True)
        probs = jnp.where(kept, jnp.exp(scores - top), 0.0).astype(BF16)
        total = jnp.sum(probs.astype(F32), axis=1, keepdims=True)
        v.probs[r] = probs
        stats = jnp.where(at_col == r, top, jnp.where(at_col == r + 8, total, stats))
    stats = stats.T[:16, :]

    for r in range(8):
        num = dot(v.probs[r], v.cv[r, :512, :], ((1,), (1,)))
        v.a1snd[r] = jnp.where(core == 0, num[64:], num[:64]).astype(BF16)
        v.a1own[r] = jnp.where(core == 0, num[:64], num[64:])
    v.st1[g] = stats
    pl.semaphore_wait(barrier, len(partners))
    s1 = {k: push("s1", k, v.st1.at[g], v.st1.at[g], at_g(k)) for k in (4,) + far_g[:6]}
    a1 = [push("a1", r, v.a1snd.at[r], v.a1rcv.at[r], at_core()) for r in range(8)]

    def joined(ref):
        peak = ref[0, :8, :]
        for i in range(1, 8):
            peak = jnp.maximum(peak, ref[i, :8, :])
        total = jnp.zeros((8, 128), F32)
        for i in range(8):
            total += ref[i, 8:, :] * jnp.exp(ref[i, :8, :] - peak)
        return peak, total

    def pair_top(x):
        return jnp.maximum(v.st1[x, :8, :], v.st1[4 + x, :8, :])

    s1.pop(4).wait_recv()
    pair = pair_top(dev)
    here = jnp.exp(v.st1[g, :8, :] - pair)
    there = jnp.exp(v.st1[other * 4 + dev, :8, :] - pair)
    v.fcol[...] = jnp.concatenate([here, there, jnp.zeros((112, 128), F32)], axis=0).T

    half = pl.ds(pl.multiple_of(core * 64, 64), 64)
    a2 = []
    for r in range(8):
        a1[r].wait_recv()
        both = v.fcol[half, r:r + 1] * v.a1own[r] + v.fcol[half, r + 8:r + 9] * v.a1rcv[r].astype(F32)
        both = both.astype(BF16)
        for x in range(4):
            v.a2snd[x, r] = both[x * 16:x * 16 + 16]
        if r % 4 == 3:
            chunk = pl.ds(r - 3, 4)
            for k in (2, 1, 3):
                xt = turn(dev, k, 4)
                a2.append(push("a2", k + r // 4 * 4, v.a2snd.at[xt, chunk], v.a2rcv.at[k, chunk], at(dev=xt)))
    for copy in s1.values():
        copy.wait_recv()
    peak, total = joined(v.st1)
    v.st2[z, :8, :] = peak
    v.st2[z, 8:, :] = total
    s2 = [push("s2", k, v.st2.at[z], v.st2.at[z], at_z(k)) for k in far_z]

    spans = ((0, 256), (128, 384), (384, 384), (640, 256))
    into, outof = iota((384, 256), 1), iota((384, 256), 0)
    for i, (first, _) in enumerate(spans):
        source = i * 224 - first + lax.div(into, 128) * 112 + lax.rem(into, 128)
        v.select[i] = one_hot((outof == source) & (lax.rem(into, 128) < 112))

    def lay_out(blocks):
        for zt in blocks:
            for i, (first, width) in enumerate(spans):
                columns = v.wdv[:, zt * 896 + first:zt * 896 + first + width]
                piece = dot(columns, v.select[i, :width, :]).astype(BF16)
                v.laid[i // 2, :, zt * 512 + i % 2 * 256:zt * 512 + i % 2 * 256 + 256] = piece

    ready(fetch_wd)
    lay_out(range(4))
    for copy in s2:
        copy.wait_recv()
    peak, total = joined(v.st2)
    factors = [jnp.exp(pair_top(turn(dev, 4 - k, 4)) - peak) / total for k in range(4)]
    v.fcol[...] = jnp.concatenate(factors + [jnp.zeros((96, 128), F32)], axis=0).T

    sixteen = pl.ds(pl.multiple_of(core * 64 + dev * 16, 16), 16)
    by_z = one_hot(at_col == part_of(at_row, 1, 8) * 16 + part_of(at_row, 16, 8) * 2 + part_of(at_row, 8, 2))
    latents = jnp.zeros((128, 512), F32)
    for c in range(2):
        for copy in a2[3 * c:3 * c + 3]:
            copy.wait_recv()
        rows = []
        for r in range(4 * c, 4 * c + 4):
            row = v.fcol[sixteen, r:r + 1] * v.a2snd[dev, r].astype(F32)
            for k in range(1, 4):
                row += v.fcol[sixteen, k * 8 + r:k * 8 + r + 1] * v.a2rcv[k, r].astype(F32)
            rows.append(row.astype(BF16))
        latents += dot(by_z[:, c * 64:c * 64 + 64], jnp.concatenate(rows, axis=0))

    v.a3snd[...] = latents.astype(BF16).reshape(8, 16, 512)
    a3 = []
    for k in far_z:
        zt = turn(z, k, 8)
        a3.append((k, push("a3", k, v.a3snd.at[zt], v.a3rcv.at[k], at_z(k))))
    for i in range(8):
        for t in range(4):
            row = i * 7 + t
            v.gain[i, :8, t * 128:t * 128 + 128] = jnp.broadcast_to(gain_ref[row:row + 1, :].astype(F32), (8, 128))
            v.gain[i, 8:, t * 128:t * 128 + 128] = jnp.broadcast_to(gain_ref[row + 3:row + 4, :].astype(F32), (8, 128))
    lay_out(range(4, 8))
    mine_rows = pl.ds(pl.multiple_of(core * 128, 128), 128)
    wd = push("wd", 0, v.laid.at[other], v.down.at[mine_rows], at_core())
    keep_wd = pltpu.make_async_copy(v.laid.at[core], v.down.at[mine_rows], local.at[21])
    keep_wd.start()
    fetches.append(keep_wd)
    ready(fetch_lift, fetch_wo)
    summed = v.a3snd[z].astype(F32)
    for k, copy in a3:
        copy.wait_recv()
        summed += v.a3rcv[k].astype(F32)
    own_heads = summed.astype(BF16)
    values = jnp.concatenate([dot(own_heads, v.liftv[0])[:8], dot(own_heads, v.liftv[1])[8:]], axis=1).astype(BF16)

    def projected(i):
        upper = dot(values, v.wov[:, pl.ds(pl.multiple_of(i * 896, 128), 512)])
        lower = dot(values, v.wov[:, pl.ds(pl.multiple_of(i * 896 + 512, 128), 384)])
        return jnp.concatenate([upper, jnp.concatenate([upper[:, 384:], lower], axis=1)], axis=0)

    b1 = []
    for k in far_g:
        gt = turn(g, k, 8)
        v.b1snd[gt] = projected(gt).astype(BF16)
        b1.append((k, push("b1", k, v.b1snd.at[gt], v.b1rcv.at[k], at_g(k))))
    summed = projected(g)
    residual = jnp.concatenate(
        [
            res_ref[:, pl.ds(pl.multiple_of(g * 896, 128), 512)].astype(F32),
            res_ref[:, pl.ds(pl.multiple_of(g * 896 + 384, 128), 512)].astype(F32),
        ],
        axis=0,
    )
    for k, copy in b1:
        copy.wait_recv()
        summed += v.b1rcv[k].astype(F32)
    v.part[z] = summed.astype(BF16)
    b2 = [push("b2", k, v.part.at[z], v.part.at[z], at_z(k)) for k in far_z]
    ready(fetch_wg, fetch_wu)
    for copy in b2:
        copy.wait_recv()
    attention = v.part[0].astype(F32)
    for i in range(1, 8):
        attention += v.part[i].astype(F32)
    mine = core * 16 + node * 4 + dev
    v.state[mine] = (residual + attention).astype(BF16)

    c1, c2 = {}, []
    for i, j in far_xy:
        where = at(node=turn(node, i, 4), dev=turn(dev, j, 4))
        c1[i, j] = push("c1", i * 4 + j, v.state.at[mine], v.state.at[mine], where)
    coef = jnp.sum(jnp.where(eid_ref[...] == expert, ew_ref[...], 0.0), axis=0, keepdims=True)
    coef = jnp.sum(jnp.where(iota((32, 32), 0) == iota((32, 32), 1), coef, 0.0), axis=1, keepdims=True)
    for i in (0, 1, 3, 2):
        for j in range(4):
            if i + j > 0:
                c1[i, j].wait_recv()
        came = pl.ds(core * 16 + turn(node, 4 - i, 4) * 4, 4)
        c2.append(push("c2", i, v.state.at[came], v.state.at[came], at_core()))

    squares = [jnp.zeros((16, 512), F32) for _ in range(4)]
    upper = jnp.zeros((64, 256), F32)
    lower = jnp.zeros((64, 256), F32)
    for c in (core, other):
        for i in range(4):
            block = c * 4 + i
            for y in range(4):
                wide = v.state[c * 16 + y * 4 + i].astype(F32)
                squares[y] += wide * wide
                v.normed[i, y * 16:y * 16 + 16, :] = (wide * v.gain[block]).astype(BF16)
            first = pl.multiple_of(block * 896, 128)
            upper += dot(v.normed[i], v.wguv[pl.ds(first, 512), :])
            lower += dot(v.normed[i, :, 128:], v.wguv[pl.ds(first + 512, 384), :])
        if c is core:
            for copy in c2:
                copy.wait_recv()
    once = (iota((16, 512), 0) < 8) | (iota((16, 512), 1) >= 128)
    scale = []
    for y in range(4):
        square = jnp.sum(jnp.where(once, squares[y], 0.0), axis=1, keepdims=True)
        scale.append(lax.rsqrt((square[:8] + square[8:]) / 7168.0 + norm_eps))
    both = jnp.concatenate([upper[y * 16:y * 16 + 8] + lower[y * 16 + 8:y * 16 + 16] for y in range(4)], axis=0)
    both = both * jnp.concatenate(scale, axis=0)
    gate, up = both[:, :128], both[:, 128:]
    v.hidden[core] = (gate / (1.0 + jnp.exp(-gate)) * up * coef).astype(BF16)
    hid = push("hid", 0, v.hidden.at[core], v.hidden.at[core], at_core())

    own = v.state[lax.div(z, 4) * 16 + node * 4 + lax.rem(z, 4)]
    own = dot(own, one_hot(iota((512, 128), 0) == iota((512, 128), 1) + core * 64 + dev * 112))
    own = jnp.where(core == 0, own[:8], own[8:])

    ready(keep_wd)
    wd.wait_recv()
    hid.wait_recv()
    hidden = jnp.concatenate([v.hidden[0], v.hidden[1]], axis=1)
    for i in range(4):
        first = dot(hidden, v.down[:, i * 1024:i * 1024 + 512])
        second = dot(hidden, v.down[:, i * 1024 + 512:i * 1024 + 1024])
        for y in range(4):
            pair = jnp.concatenate([first[y * 8:y * 8 + 8], second[y * 8:y * 8 + 8]], axis=0).astype(BF16)
            for x in range(4):
                v.d2snd[y * 4 + x, i] = pair[:, x * 128:x * 128 + 128]
    d2 = []
    for i, j in far_xy:
        yt, xt = turn(node, i, 4), turn(dev, j, 4)
        d2.append((i * 4 + j, push("d2", i * 4 + j, v.d2snd.at[yt * 4 + xt], v.d2rcv.at[i * 4 + j], at(node=yt, dev=xt))))
    mixture = [v.d2snd[node * 4 + dev, i].astype(F32) for i in range(4)]
    for k, copy in reversed(d2):
        copy.wait_recv()
        for i in range(4):
            mixture[i] += v.d2rcv[k, i].astype(F32)
    for i in range(4):
        v.d3snd[2 * i] = mixture[i][:8]
        v.d3snd[2 * i + 1] = mixture[i][8:]
    d3 = []
    for k in far_z:
        d3.append((k, push("d3", k, v.d3snd.at[turn(z, k, 8)], v.d3rcv.at[k], at_z(k))))
    mixture = v.d3snd[z]
    for k, copy in reversed(d3):
        copy.wait_recv()
        mixture += v.d3rcv[k]
    out_ref[...] = (own + mixture).astype(BF16)[:, :112]

    for copy in sent:
        copy.wait_send()


def shards(queries, latent_cache, block_ids, value_lift_weight, out_weight, residual, norm_gain, expert_ids,
           expert_weights, gate_weight, up_weight, down_weight):
    vmem, anywhere = pl.BlockSpec(memory_space=pltpu.VMEM), pl.BlockSpec(memory_space=pl.ANY)
    scratch = [pltpu.VMEM(shape, dtype) for _, shape, dtype in BUFFERS]
    scratch.append(pltpu.SemaphoreType.DMA((22,)))
    for _, count in PAIRS:
        scratch += [pltpu.SemaphoreType.DMA((count,)), pltpu.SemaphoreType.DMA((count,))]
    return pl.pallas_call(
        kernel,
        out_shape=jax.ShapeDtypeStruct((8, 112), BF16),
        in_specs=[vmem] * 5 + [anywhere] * 7,
        out_specs=vmem,
        scratch_shapes=scratch,
        compiler_params=pltpu.CompilerParams(
            collective_id=0, has_side_effects=True, vmem_limit_bytes=56 * 1024 * 1024
        ),
        name="layer",
    )(
        block_ids, norm_gain.reshape(56, 128), expert_ids.T, expert_weights.T, residual,
        jnp.swapaxes(queries, 1, 2), jnp.swapaxes(latent_cache, 1, 2),
        value_lift_weight, out_weight, gate_weight, up_weight, down_weight,
    )


def solution(mesh):
    placed = (
        P("node", None, None),
        P("node", ("ctx", "dev"), None),
        P("node", None),
        P(("ctx", "dev"), None, None),
        P(("ctx", "dev"), None),
        P("node", None),
        P(),
        P(),
        P(),
        P(("node", "dev"), None, "ctx"),
        P(("node", "dev"), None, "ctx"),
        P(("node", "dev"), "ctx", None),
    )
    return jax.shard_map(
        shards, mesh=mesh, in_specs=placed, out_specs=P("node", ("ctx", "dev")), check_vma=False
    )
```

```python
import math

import jax
import jax.numpy as jnp
from jax import lax
from jax.experimental import pallas as pl
from jax.experimental.pallas import tpu as pltpu
from jax.sharding import PartitionSpec as P

MESH = pl.DeviceIdType.MESH
F32, BF16 = jnp.float32, jnp.bfloat16
score_scale = 192.0 ** (-0.5) * (0.1 * math.log(40.0) + 1.0) ** 2
floor_score = -1e30
norm_eps = 1e-06

PAIRS = (
    ("a1", 8), ("s1", 8), ("s2", 8), ("a2", 8), ("a3", 8), ("b1", 8),
    ("b2", 8), ("c1", 16), ("c2", 4), ("wd", 1), ("hid", 1), ("d2", 16), ("d3", 8),
)
BUFFERS = (
    ("ids", (8, 32), jnp.int32), ("gain_in", (56, 128), BF16), ("eid", (8, 32), jnp.int32), ("ew", (8, 32), F32),
    ("res", (8, 7168), BF16), ("qv", (8, 576, 128), BF16), ("cv", (8, 576, 256), BF16), ("liftv", (2, 512, 128), BF16),
    ("wov", (256, 7168), BF16), ("wguv", (7168, 256), BF16), ("wdv", (128, 7168), BF16),
    ("keep", (8, 256), F32), ("probs", (8, 128, 256), BF16),
    ("st1", (8, 16, 128), F32), ("st2", (8, 16, 128), F32), ("fcol", (128, 128), F32),
    ("a1own", (8, 64, 512), F32), ("a1snd", (8, 64, 512), BF16), ("a1rcv", (8, 64, 512), BF16),
    ("a2snd", (4, 8, 16, 512), BF16), ("a2rcv", (4, 8, 16, 512), BF16),
    ("a3snd", (8, 16, 512), BF16), ("a3rcv", (8, 16, 512), BF16),
    ("b1snd", (8, 16, 512), BF16), ("b1rcv", (8, 16, 512), BF16), ("part", (8, 16, 512), BF16),
    ("state", (32, 16, 512), BF16), ("normed", (4, 64, 512), BF16), ("gain", (8, 16, 512), F32),
    ("select", (4, 384, 256), BF16), ("laid", (2, 128, 4096), BF16), ("down", (256, 4096), BF16),
    ("hidden", (2, 32, 128), BF16), ("d2snd", (16, 4, 16, 128), BF16), ("d2rcv", (16, 4, 16, 128), BF16),
    ("d3snd", (8, 8, 128), F32), ("d3rcv", (8, 8, 128), F32),
)


ROWS_AT_ONCE = 4
SENT_AT_ONCE = 4
BLOCKS_AT_ONCE = 4


class Names:
    pass


def dot(a, b, dims=((1,), (0,))):
    return lax.dot_general(a, b, (dims, ((), ())), preferred_element_type=F32)


def iota(shape, dim):
    return lax.broadcasted_iota(jnp.int32, shape, dim)


def kernel(ids_hbm, gain_hbm, eid_hbm, ew_hbm, res_hbm, q_hbm, c_hbm, lift_hbm, wo_hbm, wg_hbm, wu_hbm, wd_hbm,
           out_ref, *scratch):
    v = Names()
    for (name, _, _), ref in zip(BUFFERS, scratch):
        setattr(v, name, ref)
    rest = scratch[len(BUFFERS):]
    local = rest[0]
    sems = {name: (rest[1 + 2 * i], rest[2 + 2 * i]) for i, (name, _) in enumerate(PAIRS)}

    ctx, node, dev = lax.axis_index("ctx"), lax.axis_index("node"), lax.axis_index("dev")
    z, core = lax.div(ctx, 2), lax.rem(ctx, 2)
    other = 1 - core
    g = core * 4 + dev
    shard = ctx * 4 + dev
    expert = node * 4 + dev

    def turn(a, k, n):
        return lax.rem(a + k, n)

    def at(ctx=ctx, node=node, dev=dev):
        return {"ctx": ctx, "node": node, "dev": dev}

    def at_core():
        return at(ctx=z * 2 + other)

    def at_z(k):
        return at(ctx=turn(z, k, 8) * 2 + core)

    def at_g(k):
        there = turn(g, k, 8)
        return at(ctx=z * 2 + lax.div(there, 4), dev=lax.rem(there, 4))

    def remote(name, slot, src, dst, where):
        send, recv = sems[name]
        return pltpu.make_async_remote_copy(
            src_ref=src, dst_ref=dst, send_sem=send.at[slot], recv_sem=recv.at[slot],
            device_id=where, device_id_type=MESH,
        )

    sent, fetches = [], []

    def push(*args):
        copy = remote(*args)
        copy.start()
        sent.append(copy)
        return copy

    far_z, far_g = (4, 3, 5, 2, 6, 1, 7), (2, 6, 1, 3, 5, 7, 4)

    def hops(i, j):
        return min(i, 4 - i) + min(j, 4 - j)

    far_xy = sorted(((i, j) for i in range(4) for j in range(4) if i + j), key=lambda step: -hops(*step))

    barrier = pltpu.get_barrier_semaphore()
    partners = [(min(k, 8 - k), at_z(k)) for k in far_z]
    partners += [(2 if k in (2, 6) else k % 2, at_g(k)) for k in far_g]
    partners += [(hops(i, j), at(node=turn(node, i, 4), dev=turn(dev, j, 4))) for i in range(1, 4) for j in range(4)]
    for _, where in sorted(partners, key=lambda partner: -partner[0]):
        pl.semaphore_signal(barrier, inc=1, device_id=where, device_id_type=MESH)

    def fetch_q(r):
        return pltpu.make_async_copy(q_hbm.at[r], v.qv.at[r], local.at[r])

    def fetch_c(r):
        return pltpu.make_async_copy(c_hbm.at[r], v.cv.at[r], local.at[8 + r])

    fetch_ids = pltpu.make_async_copy(ids_hbm, v.ids, local.at[22])
    fetch_ids.start()
    for i in range(8):
        fetch_q(i).start()
        fetch_c(i).start()
    fetch_gain = pltpu.make_async_copy(gain_hbm, v.gain_in, local.at[23])
    fetch_eid = pltpu.make_async_copy(eid_hbm, v.eid, local.at[24])
    fetch_ew = pltpu.make_async_copy(ew_hbm, v.ew, local.at[25])
    fetch_res = pltpu.make_async_copy(res_hbm, v.res, local.at[26])
    fetch_lift = pltpu.make_async_copy(lift_hbm, v.liftv, local.at[16])
    fetch_wo = pltpu.make_async_copy(wo_hbm, v.wov, local.at[17])
    fetch_wg = pltpu.make_async_copy(wg_hbm.at[0], v.wguv.at[:, pl.ds(0, 128)], local.at[18])
    fetch_wu = pltpu.make_async_copy(wu_hbm.at[0], v.wguv.at[:, pl.ds(128, 128)], local.at[19])
    fetch_wd = pltpu.make_async_copy(wd_hbm.at[0], v.wdv, local.at[20])
    for copy in (fetch_gain, fetch_eid, fetch_ew, fetch_res, fetch_wd, fetch_lift, fetch_wo, fetch_wg, fetch_wu):
        copy.start()
        fetches.append(copy)

    def ready(*copies):
        for copy in copies:
            fetches[:] = [other_copy for other_copy in fetches if other_copy is not copy]
            copy.wait()

    fetch_ids.wait()
    ids = v.ids[...]
    block = lax.div(iota((8, 256), 1), 64)
    keep = jnp.zeros((8, 256), F32)
    for b in range(4):
        hit = jnp.max(jnp.where(ids == shard * 4 + b, 1.0, 0.0), axis=1, keepdims=True)
        keep = jnp.where(block == b, hit, keep)
    v.keep[...] = keep

    def one_hot(hit):
        return jnp.where(hit, 1.0, 0.0).astype(BF16)

    at_row, at_col = iota((128, 128), 0), iota((128, 128), 1)

    def part_of(number, low, size):
        return lax.rem(lax.div(number, low), size)

    by_owner = one_hot(
        at_col == part_of(at_row, 2, 8) * 16 + part_of(at_row, 64, 2) * 8 + part_of(at_row, 16, 4) * 2 + part_of(at_row, 1, 2)
    )
    stats = jnp.zeros((128, 128), F32)
    for r in range(8):
        if r % ROWS_AT_ONCE == 0:
            for i in range(r, r + ROWS_AT_ONCE):
                fetch_q(i).wait()
                fetch_c(i).wait()
        kept = v.keep[r:r + 1, :] > 0.5
        heads = dot(by_owner, v.qv[r], ((1,), (1,))).astype(BF16)
        scores = dot(heads, v.cv[r]) * score_scale
        scores = jnp.where(kept, scores, floor_score)
        top = jnp.max(scores, axis=1, keepdims=True)
        probs = jnp.where(kept, jnp.exp(scores - top), 0.0).astype(BF16)
        total = jnp.sum(probs.astype(F32), axis=1, keepdims=True)
        v.probs[r] = probs
        stats = jnp.where(at_col == r, top, jnp.where(at_col == r + 8, total, stats))
    stats = stats.T[:16, :]

    v.st1[g] = stats
    pl.semaphore_wait(barrier, len(partners))
    s1 = {k: push("s1", k, v.st1.at[g], v.st1.at[g], at_g(k)) for k in (4,) + far_g[:6]}

    a1 = []
    for r in range(8):
        num = dot(v.probs[r], v.cv[r, :512, :], ((1,), (1,)))
        v.a1snd[r] = jnp.where(core == 0, num[64:], num[:64]).astype(BF16)
        v.a1own[r] = jnp.where(core == 0, num[:64], num[64:])
        if r % SENT_AT_ONCE == SENT_AT_ONCE - 1:
            for i in range(r + 1 - SENT_AT_ONCE, r + 1):
                a1.append(push("a1", i, v.a1snd.at[i], v.a1rcv.at[i], at_core()))

    def joined(ref):
        peak = ref[0, :8, :]
        for i in range(1, 8):
            peak = jnp.maximum(peak, ref[i, :8, :])
        total = jnp.zeros((8, 128), F32)
        for i in range(8):
            total += ref[i, 8:, :] * jnp.exp(ref[i, :8, :] - peak)
        return peak, total

    def pair_top(x):
        return jnp.maximum(v.st1[x, :8, :], v.st1[4 + x, :8, :])

    s1.pop(4).wait_recv()
    pair = pair_top(dev)
    here = jnp.exp(v.st1[g, :8, :] - pair)
    there = jnp.exp(v.st1[other * 4 + dev, :8, :] - pair)
    v.fcol[...] = jnp.concatenate([here, there, jnp.zeros((112, 128), F32)], axis=0).T

    half = pl.ds(pl.multiple_of(core * 64, 64), 64)
    a2 = []
    for r in range(8):
        if r % 4 == 0:
            for copy in a1[r:r + 4]:
                copy.wait_recv()
        both = v.fcol[half, r:r + 1] * v.a1own[r] + v.fcol[half, r + 8:r + 9] * v.a1rcv[r].astype(F32)
        both = both.astype(BF16)
        for x in range(4):
            v.a2snd[x, r] = both[x * 16:x * 16 + 16]
        if r % 4 == 3:
            chunk = pl.ds(r - 3, 4)
            for k in (2, 1, 3):
                xt = turn(dev, k, 4)
                a2.append(push("a2", k + r // 4 * 4, v.a2snd.at[xt, chunk], v.a2rcv.at[k, chunk], at(dev=xt)))
    ready(fetch_gain)
    for i in range(8):
        for t in range(4):
            row = i * 7 + t
            v.gain[i, :8, t * 128:t * 128 + 128] = jnp.broadcast_to(v.gain_in[row:row + 1, :].astype(F32), (8, 128))
            v.gain[i, 8:, t * 128:t * 128 + 128] = jnp.broadcast_to(v.gain_in[row + 3:row + 4, :].astype(F32), (8, 128))

    spans = ((0, 256), (128, 384), (384, 384), (640, 256))
    into, outof = iota((384, 256), 1), iota((384, 256), 0)
    for i, (first, _) in enumerate(spans):
        source = i * 224 - first + lax.div(into, 128) * 112 + lax.rem(into, 128)
        v.select[i] = one_hot((outof == source) & (lax.rem(into, 128) < 112))

    def lay_out(blocks):
        for zt in blocks:
            for i, (first, width) in enumerate(spans):
                columns = v.wdv[:, zt * 896 + first:zt * 896 + first + width]
                piece = dot(columns, v.select[i, :width, :]).astype(BF16)
                v.laid[i // 2, :, zt * 512 + i % 2 * 256:zt * 512 + i % 2 * 256 + 256] = piece

    for copy in s1.values():
        copy.wait_recv()
    peak, total = joined(v.st1)
    v.st2[z, :8, :] = peak
    v.st2[z, 8:, :] = total
    s2 = [push("s2", k, v.st2.at[z], v.st2.at[z], at_z(k)) for k in far_z]

    factors = [jnp.exp(pair_top(turn(dev, 4 - k, 4)) - peak) for k in range(4)]
    v.fcol[...] = jnp.concatenate(factors + [jnp.zeros((96, 128), F32)], axis=0).T
    ready(fetch_wd)
    lay_out(range(2))

    sixteen = pl.ds(pl.multiple_of(core * 64 + dev * 16, 16), 16)
    by_z = one_hot(at_col == part_of(at_row, 1, 8) * 16 + part_of(at_row, 16, 8) * 2 + part_of(at_row, 8, 2))
    latents = jnp.zeros((128, 512), F32)
    for c in range(2):
        for copy in a2[3 * c:3 * c + 3]:
            copy.wait_recv()
        rows = []
        for r in range(4 * c, 4 * c + 4):
            row = v.fcol[sixteen, r:r + 1] * v.a2snd[dev, r].astype(F32)
            for k in range(1, 4):
                row += v.fcol[sixteen, k * 8 + r:k * 8 + r + 1] * v.a2rcv[k, r].astype(F32)
            rows.append(row.astype(BF16))
        latents += dot(by_z[:, c * 64:c * 64 + 64], jnp.concatenate(rows, axis=0))

    v.a3snd[...] = latents.astype(BF16).reshape(8, 16, 512)
    a3 = []
    for k in far_z:
        zt = turn(z, k, 8)
        a3.append((k, push("a3", k, v.a3snd.at[zt], v.a3rcv.at[k], at_z(k))))
    lay_out(range(2, 5))
    ready(fetch_lift, fetch_wo)
    for copy in s2:
        copy.wait_recv()
    peak, total = joined(v.st2)

    own_lane = iota((8, 128), 1) - (core * 64 + dev * 16 + z * 2)

    def factor_of(zt):
        factor = jnp.exp(v.st2[zt, :8, :] - peak) / total
        columns = [jnp.sum(jnp.where(own_lane == h, factor, 0.0), axis=1, keepdims=True) for h in range(2)]
        return jnp.concatenate(columns, axis=0)

    factors = [factor_of(turn(z, 8 - k, 8)) for k in range(8)]
    summed = factors[0] * v.a3snd[z].astype(F32)
    for _, copy in reversed(a3):
        copy.wait_recv()
    for k in range(1, 8):
        summed += factors[k] * v.a3rcv[k].astype(F32)
    own_heads = summed.astype(BF16)
    values = jnp.concatenate([dot(own_heads, v.liftv[0])[:8], dot(own_heads, v.liftv[1])[8:]], axis=1).astype(BF16)

    def projected(i):
        upper = dot(values, v.wov[:, pl.ds(pl.multiple_of(i * 896, 128), 512)])
        lower = dot(values, v.wov[:, pl.ds(pl.multiple_of(i * 896 + 512, 128), 384)])
        return jnp.concatenate([upper, jnp.concatenate([upper[:, 384:], lower], axis=1)], axis=0)

    b1 = []
    for i in range(0, 7, BLOCKS_AT_ONCE):
        for k in far_g[i:i + BLOCKS_AT_ONCE]:
            gt = turn(g, k, 8)
            v.b1snd[gt] = projected(gt).astype(BF16)
        for k in far_g[i:i + BLOCKS_AT_ONCE]:
            b1.append((k, push("b1", k, v.b1snd.at[turn(g, k, 8)], v.b1rcv.at[k], at_g(k))))
    summed = projected(g)
    ready(fetch_res)
    residual = jnp.concatenate(
        [
            v.res[:, pl.ds(pl.multiple_of(g * 896, 128), 512)].astype(F32),
            v.res[:, pl.ds(pl.multiple_of(g * 896 + 384, 128), 512)].astype(F32),
        ],
        axis=0,
    )
    for _, copy in reversed(b1):
        copy.wait_recv()
    for k in range(1, 8):
        summed += v.b1rcv[k].astype(F32)
    v.part[z] = summed.astype(BF16)
    b2 = [push("b2", k, v.part.at[z], v.part.at[z], at_z(k)) for k in far_z]
    lay_out(range(5, 8))
    mine_rows = pl.ds(pl.multiple_of(core * 128, 128), 128)
    wd = push("wd", 0, v.laid.at[other], v.down.at[mine_rows], at_core())
    keep_wd = pltpu.make_async_copy(v.laid.at[core], v.down.at[mine_rows], local.at[21])
    keep_wd.start()
    fetches.append(keep_wd)
    ready(fetch_wg, fetch_wu)
    for copy in b2:
        copy.wait_recv()
    attention = v.part[0].astype(F32)
    for i in range(1, 8):
        attention += v.part[i].astype(F32)
    mine = core * 16 + node * 4 + dev
    v.state[mine] = (residual + attention).astype(BF16)

    c1, c2 = {}, []
    for i, j in far_xy:
        where = at(node=turn(node, i, 4), dev=turn(dev, j, 4))
        c1[i, j] = push("c1", i * 4 + j, v.state.at[mine], v.state.at[mine], where)
    ready(fetch_eid, fetch_ew)
    coef = jnp.sum(jnp.where(v.eid[...] == expert, v.ew[...], 0.0), axis=0, keepdims=True)
    coef = jnp.sum(jnp.where(iota((32, 32), 0) == iota((32, 32), 1), coef, 0.0), axis=1, keepdims=True)
    for i in (0, 1, 3, 2):
        for j in range(4):
            if i + j > 0:
                c1[i, j].wait_recv()
        came = pl.ds(core * 16 + turn(node, 4 - i, 4) * 4, 4)
        c2.append(push("c2", i, v.state.at[came], v.state.at[came], at_core()))

    squares = [jnp.zeros((16, 512), F32) for _ in range(4)]
    upper = jnp.zeros((64, 256), F32)
    lower = jnp.zeros((64, 256), F32)
    for c in (core, other):
        for i in range(4):
            block = c * 4 + i
            for y in range(4):
                wide = v.state[c * 16 + y * 4 + i].astype(F32)
                squares[y] += wide * wide
                v.normed[i, y * 16:y * 16 + 16, :] = (wide * v.gain[block]).astype(BF16)
            first = pl.multiple_of(block * 896, 128)
            upper += dot(v.normed[i], v.wguv[pl.ds(first, 512), :])
            lower += dot(v.normed[i, :, 128:], v.wguv[pl.ds(first + 512, 384), :])
        if c is core:
            for copy in c2:
                copy.wait_recv()
    once = (iota((16, 512), 0) < 8) | (iota((16, 512), 1) >= 128)
    scale = []
    for y in range(4):
        square = jnp.sum(jnp.where(once, squares[y], 0.0), axis=1, keepdims=True)
        scale.append(lax.rsqrt((square[:8] + square[8:]) / 7168.0 + norm_eps))
    both = jnp.concatenate([upper[y * 16:y * 16 + 8] + lower[y * 16 + 8:y * 16 + 16] for y in range(4)], axis=0)
    both = both * jnp.concatenate(scale, axis=0)
    gate, up = both[:, :128], both[:, 128:]
    v.hidden[core] = (gate / (1.0 + jnp.exp(-gate)) * up * coef).astype(BF16)
    hid = push("hid", 0, v.hidden.at[core], v.hidden.at[core], at_core())

    own = v.state[lax.div(z, 4) * 16 + node * 4 + lax.rem(z, 4)]
    own = dot(own, one_hot(iota((512, 128), 0) == iota((512, 128), 1) + core * 64 + dev * 112))
    own = jnp.where(core == 0, own[:8], own[8:])

    ready(keep_wd)
    wd.wait_recv()
    hid.wait_recv()
    hidden = jnp.concatenate([v.hidden[0], v.hidden[1]], axis=1)
    for i in range(4):
        first = dot(hidden, v.down[:, i * 1024:i * 1024 + 512])
        second = dot(hidden, v.down[:, i * 1024 + 512:i * 1024 + 1024])
        for y in range(4):
            pair = jnp.concatenate([first[y * 8:y * 8 + 8], second[y * 8:y * 8 + 8]], axis=0).astype(BF16)
            for x in range(4):
                v.d2snd[y * 4 + x, i] = pair[:, x * 128:x * 128 + 128]
    d2 = []
    for i, j in far_xy:
        yt, xt = turn(node, i, 4), turn(dev, j, 4)
        d2.append((i * 4 + j, push("d2", i * 4 + j, v.d2snd.at[yt * 4 + xt], v.d2rcv.at[i * 4 + j], at(node=yt, dev=xt))))
    mixture = [v.d2snd[node * 4 + dev, i].astype(F32) for i in range(4)]
    for _, copy in reversed(d2):
        copy.wait_recv()
    for k in range(1, 16):
        for i in range(4):
            mixture[i] += v.d2rcv[k, i].astype(F32)
    for i in range(4):
        v.d3snd[2 * i] = mixture[i][:8]
        v.d3snd[2 * i + 1] = mixture[i][8:]
    d3 = []
    for k in far_z:
        d3.append((k, push("d3", k, v.d3snd.at[turn(z, k, 8)], v.d3rcv.at[k], at_z(k))))
    mixture = v.d3snd[z]
    for _, copy in reversed(d3):
        copy.wait_recv()
    for k in range(1, 8):
        mixture += v.d3rcv[k]
    out_ref[...] = (own + mixture).astype(BF16)[:, :112]

    for copy in sent:
        copy.wait_send()


def shards(queries, latent_cache, block_ids, value_lift_weight, out_weight, residual, norm_gain, expert_ids,
           expert_weights, gate_weight, up_weight, down_weight):
    vmem, anywhere = pl.BlockSpec(memory_space=pltpu.VMEM), pl.BlockSpec(memory_space=pl.ANY)
    scratch = [pltpu.VMEM(shape, dtype) for _, shape, dtype in BUFFERS]
    scratch.append(pltpu.SemaphoreType.DMA((27,)))
    for _, count in PAIRS:
        scratch += [pltpu.SemaphoreType.DMA((count,)), pltpu.SemaphoreType.DMA((count,))]
    return pl.pallas_call(
        kernel,
        out_shape=jax.ShapeDtypeStruct((8, 112), BF16),
        in_specs=[anywhere] * 12,
        out_specs=vmem,
        scratch_shapes=scratch,
        compiler_params=pltpu.CompilerParams(
            collective_id=0, has_side_effects=True, vmem_limit_bytes=56 * 1024 * 1024
        ),
        name="layer",
    )(
        block_ids, norm_gain.reshape(56, 128), expert_ids.T, expert_weights.T, residual,
        jnp.swapaxes(queries, 1, 2), jnp.swapaxes(latent_cache, 1, 2),
        value_lift_weight, out_weight, gate_weight, up_weight, down_weight,
    )


def solution(mesh):
    placed = (
        P("node", None, None),
        P("node", ("ctx", "dev"), None),
        P("node", None),
        P(("ctx", "dev"), None, None),
        P(("ctx", "dev"), None),
        P("node", None),
        P(),
        P(),
        P(),
        P(("node", "dev"), None, "ctx"),
        P(("node", "dev"), None, "ctx"),
        P(("node", "dev"), "ctx", None),
    )
    return jax.shard_map(
        shards, mesh=mesh, in_specs=placed, out_specs=P("node", ("ctx", "dev")), check_vma=False
    )
```

```python
import math

import jax
import jax.numpy as jnp
from jax import lax
from jax.experimental import pallas as pl
from jax.experimental.pallas import tpu as pltpu
from jax.sharding import PartitionSpec as P

MESH = pl.DeviceIdType.MESH
F32, BF16 = jnp.float32, jnp.bfloat16
score_scale = 192.0 ** (-0.5) * (0.1 * math.log(40.0) + 1.0) ** 2
floor_score = -1e30
norm_eps = 1e-06

PAIRS = (
    ("a1", 8), ("s1", 8), ("s2", 8), ("a2", 8), ("a3", 8), ("e1", 8), ("e2", 4), ("b1", 8),
    ("b2", 8), ("c1", 16), ("c2", 4), ("wd", 1), ("hid", 1), ("d2", 16), ("d3", 8),
)
BUFFERS = (
    ("ids", (8, 32), jnp.int32), ("gain_in", (56, 128), BF16), ("eid", (8, 32), jnp.int32), ("ew", (8, 32), F32),
    ("res", (8, 7168), BF16), ("qv", (8, 576, 128), BF16), ("cv", (8, 576, 256), BF16), ("liftv", (2, 512, 128), BF16),
    ("wov", (256, 7168), BF16), ("wguv", (7168, 256), BF16), ("wdv", (128, 7168), BF16),
    ("keep", (8, 256), F32), ("probs", (8, 128, 256), BF16),
    ("st1", (8, 16, 128), F32), ("st2", (8, 24, 128), F32), ("fcol", (128, 128), F32),
    ("a1own", (8, 64, 512), F32), ("a1snd", (8, 64, 512), BF16), ("a1rcv", (8, 64, 512), BF16),
    ("a2snd", (4, 6, 16, 512), BF16), ("a2rcv", (4, 6, 16, 512), BF16),
    ("e1snd", (8, 16, 512), BF16), ("e1rcv", (8, 16, 512), BF16), ("e2snd", (4, 16, 512), BF16), ("e2rcv", (4, 16, 512), BF16),
    ("a3snd", (8, 16, 512), BF16), ("a3rcv", (8, 16, 512), BF16),
    ("b1snd", (8, 16, 512), BF16), ("b1rcv", (8, 16, 512), BF16), ("part", (8, 16, 512), BF16),
    ("state", (32, 16, 512), BF16), ("normed", (4, 64, 512), BF16), ("gain", (8, 16, 512), F32),
    ("select", (4, 384, 256), BF16), ("laid", (2, 128, 4096), BF16), ("down", (256, 4096), BF16),
    ("hidden", (2, 32, 128), BF16), ("d2snd", (16, 4, 16, 128), BF16), ("d2rcv", (16, 4, 16, 128), BF16),
    ("d3snd", (8, 8, 128), F32), ("d3rcv", (8, 8, 128), F32),
)


ROWS_AT_ONCE = 4
SENT_AT_ONCE = 4
BLOCKS_AT_ONCE = 4


class Names:
    pass


def dot(a, b, dims=((1,), (0,))):
    return lax.dot_general(a, b, (dims, ((), ())), preferred_element_type=F32)


def iota(shape, dim):
    return lax.broadcasted_iota(jnp.int32, shape, dim)


def kernel(ids_hbm, gain_hbm, eid_hbm, ew_hbm, res_hbm, q_hbm, c_hbm, lift_hbm, wo_hbm, wg_hbm, wu_hbm, wd_hbm,
           out_ref, *scratch):
    v = Names()
    for (name, _, _), ref in zip(BUFFERS, scratch):
        setattr(v, name, ref)
    rest = scratch[len(BUFFERS):]
    local = rest[0]
    sems = {name: (rest[1 + 2 * i], rest[2 + 2 * i]) for i, (name, _) in enumerate(PAIRS)}

    ctx, node, dev = lax.axis_index("ctx"), lax.axis_index("node"), lax.axis_index("dev")
    z, core = lax.div(ctx, 2), lax.rem(ctx, 2)
    other = 1 - core
    g = core * 4 + dev
    shard = ctx * 4 + dev
    expert = node * 4 + dev

    def turn(a, k, n):
        return lax.rem(a + k, n)

    def at(ctx=ctx, node=node, dev=dev):
        return {"ctx": ctx, "node": node, "dev": dev}

    def at_core():
        return at(ctx=z * 2 + other)

    def at_z(k):
        return at(ctx=turn(z, k, 8) * 2 + core)

    def at_g(k):
        there = turn(g, k, 8)
        return at(ctx=z * 2 + lax.div(there, 4), dev=lax.rem(there, 4))

    def remote(name, slot, src, dst, where):
        send, recv = sems[name]
        return pltpu.make_async_remote_copy(
            src_ref=src, dst_ref=dst, send_sem=send.at[slot], recv_sem=recv.at[slot],
            device_id=where, device_id_type=MESH,
        )

    sent, fetches = [], []

    def push(*args):
        copy = remote(*args)
        copy.start()
        sent.append(copy)
        return copy

    far_z, far_g = (4, 3, 5, 2, 6, 1, 7), (2, 6, 1, 3, 5, 7, 4)

    def hops(i, j):
        return min(i, 4 - i) + min(j, 4 - j)

    far_xy = sorted(((i, j) for i in range(4) for j in range(4) if i + j), key=lambda step: -hops(*step))

    barrier = pltpu.get_barrier_semaphore()
    partners = [(min(k, 8 - k), at_z(k)) for k in far_z]
    partners += [(2 if k in (2, 6) else k % 2, at_g(k)) for k in far_g]
    partners += [(hops(i, j), at(node=turn(node, i, 4), dev=turn(dev, j, 4))) for i in range(1, 4) for j in range(4)]
    for _, where in sorted(partners, key=lambda partner: -partner[0]):
        pl.semaphore_signal(barrier, inc=1, device_id=where, device_id_type=MESH)

    def fetch_q(r):
        return pltpu.make_async_copy(q_hbm.at[r], v.qv.at[r], local.at[r])

    def fetch_c(r):
        return pltpu.make_async_copy(c_hbm.at[r], v.cv.at[r], local.at[8 + r])

    fetch_ids = pltpu.make_async_copy(ids_hbm, v.ids, local.at[22])
    fetch_ids.start()
    for i in range(8):
        fetch_q(i).start()
        fetch_c(i).start()
    fetch_gain = pltpu.make_async_copy(gain_hbm, v.gain_in, local.at[23])
    fetch_eid = pltpu.make_async_copy(eid_hbm, v.eid, local.at[24])
    fetch_ew = pltpu.make_async_copy(ew_hbm, v.ew, local.at[25])
    fetch_res = pltpu.make_async_copy(res_hbm, v.res, local.at[26])
    fetch_lift = pltpu.make_async_copy(lift_hbm, v.liftv, local.at[16])
    fetch_wo = pltpu.make_async_copy(wo_hbm, v.wov, local.at[17])
    fetch_wg = pltpu.make_async_copy(wg_hbm.at[0], v.wguv.at[:, pl.ds(0, 128)], local.at[18])
    fetch_wu = pltpu.make_async_copy(wu_hbm.at[0], v.wguv.at[:, pl.ds(128, 128)], local.at[19])
    fetch_wd = pltpu.make_async_copy(wd_hbm.at[0], v.wdv, local.at[20])
    for copy in (fetch_gain, fetch_eid, fetch_ew, fetch_res, fetch_wd, fetch_lift, fetch_wo, fetch_wg, fetch_wu):
        copy.start()
        fetches.append(copy)

    def ready(*copies):
        for copy in copies:
            fetches[:] = [other_copy for other_copy in fetches if other_copy is not copy]
            copy.wait()

    fetch_ids.wait()
    ids = v.ids[...]
    block = lax.div(iota((8, 256), 1), 64)
    keep = jnp.zeros((8, 256), F32)
    for b in range(4):
        hit = jnp.max(jnp.where(ids == shard * 4 + b, 1.0, 0.0), axis=1, keepdims=True)
        keep = jnp.where(block == b, hit, keep)
    v.keep[...] = keep

    def one_hot(hit):
        return jnp.where(hit, 1.0, 0.0).astype(BF16)

    at_row, at_col = iota((128, 128), 0), iota((128, 128), 1)

    def part_of(number, low, size):
        return lax.rem(lax.div(number, low), size)

    by_owner = one_hot(
        at_col == part_of(at_row, 2, 8) * 16 + part_of(at_row, 64, 2) * 8 + part_of(at_row, 16, 4) * 2 + part_of(at_row, 1, 2)
    )
    stats = jnp.zeros((128, 128), F32)
    for r in range(8):
        if r % ROWS_AT_ONCE == 0:
            for i in range(r, r + ROWS_AT_ONCE):
                fetch_q(i).wait()
                fetch_c(i).wait()
        kept = v.keep[r:r + 1, :] > 0.5
        heads = dot(by_owner, v.qv[r], ((1,), (1,))).astype(BF16)
        scores = dot(heads, v.cv[r]) * score_scale
        scores = jnp.where(kept, scores, floor_score)
        top = jnp.max(scores, axis=1, keepdims=True)
        probs = jnp.where(kept, jnp.exp(scores - top), 0.0).astype(BF16)
        total = jnp.sum(probs.astype(F32), axis=1, keepdims=True)
        v.probs[r] = probs
        stats = jnp.where(at_col == r, top, jnp.where(at_col == r + 8, total, stats))
    stats = stats.T[:16, :]

    v.st1[g] = stats
    pl.semaphore_wait(barrier, len(partners))
    s1 = {k: push("s1", k, v.st1.at[g], v.st1.at[g], at_g(k)) for k in (4,) + far_g[:6]}

    a1 = []
    for r in range(8):
        num = dot(v.probs[r], v.cv[r, :512, :], ((1,), (1,)))
        v.a1snd[r] = jnp.where(core == 0, num[64:], num[:64]).astype(BF16)
        v.a1own[r] = jnp.where(core == 0, num[:64], num[64:])
        if r % SENT_AT_ONCE == SENT_AT_ONCE - 1:
            for i in range(r + 1 - SENT_AT_ONCE, r + 1):
                a1.append(push("a1", i, v.a1snd.at[i], v.a1rcv.at[i], at_core()))

    def joined(ref):
        peak = ref[0, :8, :]
        for i in range(1, 8):
            peak = jnp.maximum(peak, ref[i, :8, :])
        total = jnp.zeros((8, 128), F32)
        for i in range(8):
            total += ref[i, 8:16, :] * jnp.exp(ref[i, :8, :] - peak)
        return peak, total

    def pair_top(x):
        return jnp.maximum(v.st1[x, :8, :], v.st1[4 + x, :8, :])

    s1.pop(4).wait_recv()
    pair = pair_top(dev)
    here = jnp.exp(v.st1[g, :8, :] - pair)
    there = jnp.exp(v.st1[other * 4 + dev, :8, :] - pair)
    v.fcol[...] = jnp.concatenate([here, there, jnp.zeros((112, 128), F32)], axis=0).T

    half = pl.ds(pl.multiple_of(core * 64, 64), 64)

    def core_join(r):
        both = v.fcol[half, r:r + 1] * v.a1own[r] + v.fcol[half, r + 8:r + 9] * v.a1rcv[r].astype(F32)
        return both.astype(BF16)

    a2 = []
    for c in range(2):
        for copy in a1[3 * c:3 * c + 3]:
            copy.wait_recv()
        for r in range(3 * c, 3 * c + 3):
            both = core_join(r)
            for x in range(4):
                v.a2snd[x, r] = both[x * 16:x * 16 + 16]
        chunk = pl.ds(3 * c, 3)
        for k in (2, 1, 3):
            xt = turn(dev, k, 4)
            a2.append(push("a2", k + c * 4, v.a2snd.at[xt, chunk], v.a2rcv.at[k, chunk], at(dev=xt)))
    for copy in a1[6:]:
        copy.wait_recv()
    to_z = one_hot(
        at_col == part_of(at_row, 1, 2) * 64 + part_of(at_row, 4, 4) * 16 + part_of(at_row, 16, 8) * 2 + part_of(at_row, 2, 2)
    )
    late = dot(to_z, jnp.concatenate([core_join(6), core_join(7)], axis=0))
    v.e1snd[...] = late.astype(BF16).reshape(8, 16, 512)
    e1 = [push("e1", k, v.e1snd.at[turn(z, k, 8)], v.e1rcv.at[k], at_z(k)) for k in far_z]
    ready(fetch_gain)
    for i in range(8):
        for t in range(4):
            row = i * 7 + t
            v.gain[i, :8, t * 128:t * 128 + 128] = jnp.broadcast_to(v.gain_in[row:row + 1, :].astype(F32), (8, 128))
            v.gain[i, 8:, t * 128:t * 128 + 128] = jnp.broadcast_to(v.gain_in[row + 3:row + 4, :].astype(F32), (8, 128))

    spans = ((0, 256), (128, 384), (384, 384), (640, 256))
    into, outof = iota((384, 256), 1), iota((384, 256), 0)
    for i, (first, _) in enumerate(spans):
        source = i * 224 - first + lax.div(into, 128) * 112 + lax.rem(into, 128)
        v.select[i] = one_hot((outof == source) & (lax.rem(into, 128) < 112))

    def lay_out(blocks):
        for zt in blocks:
            for i, (first, width) in enumerate(spans):
                columns = v.wdv[:, zt * 896 + first:zt * 896 + first + width]
                piece = dot(columns, v.select[i, :width, :]).astype(BF16)
                v.laid[i // 2, :, zt * 512 + i % 2 * 256:zt * 512 + i % 2 * 256 + 256] = piece

    for copy in s1.values():
        copy.wait_recv()
    peak, total = joined(v.st1)
    v.st2[z, :8, :] = peak
    v.st2[z, 8:16, :] = total
    v.st2[z, 16:, :] = pair
    s2 = [push("s2", k, v.st2.at[z], v.st2.at[z], at_z(k)) for k in far_z]

    factors = [jnp.exp(pair_top(turn(dev, 4 - k, 4)) - peak) for k in range(4)]
    v.fcol[...] = jnp.concatenate(factors + [jnp.zeros((96, 128), F32)], axis=0).T
    ready(fetch_wd)
    lay_out(range(2))

    sixteen = pl.ds(pl.multiple_of(core * 64 + dev * 16, 16), 16)
    by_row, by_col = iota((128, 48), 0), iota((128, 48), 1)
    latents = jnp.zeros((128, 512), F32)
    for c in range(2):
        for copy in a2[3 * c:3 * c + 3]:
            copy.wait_recv()
        rows = []
        for r in range(3 * c, 3 * c + 3):
            row = v.fcol[sixteen, r:r + 1] * v.a2snd[dev, r].astype(F32)
            for k in range(1, 4):
                row += v.fcol[sixteen, k * 8 + r:k * 8 + r + 1] * v.a2rcv[k, r].astype(F32)
            rows.append(row.astype(BF16))
        by_z = one_hot(by_col + c * 48 == part_of(by_row, 1, 8) * 16 + part_of(by_row, 16, 8) * 2 + part_of(by_row, 8, 2))
        latents += dot(by_z, jnp.concatenate(rows, axis=0))

    v.a3snd[...] = latents.astype(BF16).reshape(8, 16, 512)
    a3 = []
    for k in far_z:
        zt = turn(z, k, 8)
        a3.append((k, push("a3", k, v.a3snd.at[zt], v.a3rcv.at[k], at_z(k))))
    for copy in s2:
        copy.wait_recv()
    peak, total = joined(v.st2)

    late_row, late_lane = iota((16, 128), 0), iota((16, 128), 1)
    late_head = late_lane == core * 64 + part_of(late_row, 4, 4) * 16 + z * 2 + part_of(late_row, 2, 2)

    def late_factor(zt):
        factor = jnp.exp(v.st2[zt, 16:, :] - peak) / total
        factor = jnp.where(part_of(late_row, 1, 2) == 0, factor[6:7], factor[7:8])
        return jnp.sum(jnp.where(late_head, factor, 0.0), axis=1, keepdims=True)

    late_factors = [late_factor(turn(z, 8 - k, 8)) for k in range(8)]
    for copy in reversed(e1):
        copy.wait_recv()
    late = late_factors[0] * v.e1snd[z].astype(F32)
    for k in range(1, 8):
        late += late_factors[k] * v.e1rcv[k].astype(F32)
    to_row, to_col = iota((64, 16), 0), iota((64, 16), 1)
    to_x = one_hot(
        (part_of(to_row, 1, 8) >= 6)
        & (to_col == part_of(to_row, 16, 4) * 4 + part_of(to_row, 8, 2) * 2 + part_of(to_row, 1, 8) - 6)
    )
    v.e2snd[...] = dot(to_x, late.astype(BF16)).astype(BF16).reshape(4, 16, 512)
    e2 = [push("e2", k, v.e2snd.at[turn(dev, k, 4)], v.e2rcv.at[k], at(dev=turn(dev, k, 4))) for k in (2, 1, 3)]
    lay_out(range(2, 5))
    ready(fetch_lift, fetch_wo)

    own_lane = iota((8, 128), 1) - (core * 64 + dev * 16 + z * 2)

    def factor_of(zt):
        factor = jnp.exp(v.st2[zt, :8, :] - peak) / total
        columns = [jnp.sum(jnp.where(own_lane == h, factor, 0.0), axis=1, keepdims=True) for h in range(2)]
        return jnp.concatenate(columns, axis=0)

    factors = [factor_of(turn(z, 8 - k, 8)) for k in range(8)]
    summed = factors[0] * v.a3snd[z].astype(F32)
    for _, copy in reversed(a3):
        copy.wait_recv()
    for k in range(1, 8):
        summed += factors[k] * v.a3rcv[k].astype(F32)
    for copy in e2:
        copy.wait_recv()
    summed += v.e2snd[dev].astype(F32)
    for k in range(1, 4):
        summed += v.e2rcv[k].astype(F32)
    own_heads = summed.astype(BF16)
    values = jnp.concatenate([dot(own_heads, v.liftv[0])[:8], dot(own_heads, v.liftv[1])[8:]], axis=1).astype(BF16)

    def projected(i):
        upper = dot(values, v.wov[:, pl.ds(pl.multiple_of(i * 896, 128), 512)])
        lower = dot(values, v.wov[:, pl.ds(pl.multiple_of(i * 896 + 512, 128), 384)])
        return jnp.concatenate([upper, jnp.concatenate([upper[:, 384:], lower], axis=1)], axis=0)

    b1 = []
    for i in range(0, 7, BLOCKS_AT_ONCE):
        for k in far_g[i:i + BLOCKS_AT_ONCE]:
            gt = turn(g, k, 8)
            v.b1snd[gt] = projected(gt).astype(BF16)
        for k in far_g[i:i + BLOCKS_AT_ONCE]:
            b1.append((k, push("b1", k, v.b1snd.at[turn(g, k, 8)], v.b1rcv.at[k], at_g(k))))
    summed = projected(g)
    ready(fetch_res)
    residual = jnp.concatenate(
        [
            v.res[:, pl.ds(pl.multiple_of(g * 896, 128), 512)].astype(F32),
            v.res[:, pl.ds(pl.multiple_of(g * 896 + 384, 128), 512)].astype(F32),
        ],
        axis=0,
    )
    for _, copy in reversed(b1):
        copy.wait_recv()
    for k in range(1, 8):
        summed += v.b1rcv[k].astype(F32)
    v.part[z] = summed.astype(BF16)
    b2 = [push("b2", k, v.part.at[z], v.part.at[z], at_z(k)) for k in far_z]
    lay_out(range(5, 8))
    mine_rows = pl.ds(pl.multiple_of(core * 128, 128), 128)
    wd = push("wd", 0, v.laid.at[other], v.down.at[mine_rows], at_core())
    keep_wd = pltpu.make_async_copy(v.laid.at[core], v.down.at[mine_rows], local.at[21])
    keep_wd.start()
    fetches.append(keep_wd)
    ready(fetch_wg, fetch_wu)
    for copy in b2:
        copy.wait_recv()
    attention = v.part[0].astype(F32)
    for i in range(1, 8):
        attention += v.part[i].astype(F32)
    mine = core * 16 + node * 4 + dev
    v.state[mine] = (residual + attention).astype(BF16)

    c1, c2 = {}, []
    for i, j in far_xy:
        where = at(node=turn(node, i, 4), dev=turn(dev, j, 4))
        c1[i, j] = push("c1", i * 4 + j, v.state.at[mine], v.state.at[mine], where)
    ready(fetch_eid, fetch_ew)
    coef = jnp.sum(jnp.where(v.eid[...] == expert, v.ew[...], 0.0), axis=0, keepdims=True)
    coef = jnp.sum(jnp.where(iota((32, 32), 0) == iota((32, 32), 1), coef, 0.0), axis=1, keepdims=True)
    for i in (0, 1, 3, 2):
        for j in range(4):
            if i + j > 0:
                c1[i, j].wait_recv()
        came = pl.ds(core * 16 + turn(node, 4 - i, 4) * 4, 4)
        c2.append(push("c2", i, v.state.at[came], v.state.at[came], at_core()))

    squares = [jnp.zeros((16, 512), F32) for _ in range(4)]
    upper = jnp.zeros((64, 256), F32)
    lower = jnp.zeros((64, 256), F32)
    for c in (core, other):
        for i in range(4):
            block = c * 4 + i
            for y in range(4):
                wide = v.state[c * 16 + y * 4 + i].astype(F32)
                squares[y] += wide * wide
                v.normed[i, y * 16:y * 16 + 16, :] = (wide * v.gain[block]).astype(BF16)
            first = pl.multiple_of(block * 896, 128)
            upper += dot(v.normed[i], v.wguv[pl.ds(first, 512), :])
            lower += dot(v.normed[i, :, 128:], v.wguv[pl.ds(first + 512, 384), :])
        if c is core:
            for copy in c2:
                copy.wait_recv()
    once = (iota((16, 512), 0) < 8) | (iota((16, 512), 1) >= 128)
    scale = []
    for y in range(4):
        square = jnp.sum(jnp.where(once, squares[y], 0.0), axis=1, keepdims=True)
        scale.append(lax.rsqrt((square[:8] + square[8:]) / 7168.0 + norm_eps))
    both = jnp.concatenate([upper[y * 16:y * 16 + 8] + lower[y * 16 + 8:y * 16 + 16] for y in range(4)], axis=0)
    both = both * jnp.concatenate(scale, axis=0)
    gate, up = both[:, :128], both[:, 128:]
    v.hidden[core] = (gate / (1.0 + jnp.exp(-gate)) * up * coef).astype(BF16)
    hid = push("hid", 0, v.hidden.at[core], v.hidden.at[core], at_core())

    own = v.state[lax.div(z, 4) * 16 + node * 4 + lax.rem(z, 4)]
    own = dot(own, one_hot(iota((512, 128), 0) == iota((512, 128), 1) + core * 64 + dev * 112))
    own = jnp.where(core == 0, own[:8], own[8:])

    ready(keep_wd)
    wd.wait_recv()
    hid.wait_recv()
    hidden = jnp.concatenate([v.hidden[0], v.hidden[1]], axis=1)
    for i in range(4):
        first = dot(hidden, v.down[:, i * 1024:i * 1024 + 512])
        second = dot(hidden, v.down[:, i * 1024 + 512:i * 1024 + 1024])
        for y in range(4):
            pair = jnp.concatenate([first[y * 8:y * 8 + 8], second[y * 8:y * 8 + 8]], axis=0).astype(BF16)
            for x in range(4):
                v.d2snd[y * 4 + x, i] = pair[:, x * 128:x * 128 + 128]
    d2 = []
    for i, j in far_xy:
        yt, xt = turn(node, i, 4), turn(dev, j, 4)
        d2.append((i * 4 + j, push("d2", i * 4 + j, v.d2snd.at[yt * 4 + xt], v.d2rcv.at[i * 4 + j], at(node=yt, dev=xt))))
    mixture = [v.d2snd[node * 4 + dev, i].astype(F32) for i in range(4)]
    for _, copy in reversed(d2):
        copy.wait_recv()
    for k in range(1, 16):
        for i in range(4):
            mixture[i] += v.d2rcv[k, i].astype(F32)
    for i in range(4):
        v.d3snd[2 * i] = mixture[i][:8]
        v.d3snd[2 * i + 1] = mixture[i][8:]
    d3 = []
    for k in far_z:
        d3.append((k, push("d3", k, v.d3snd.at[turn(z, k, 8)], v.d3rcv.at[k], at_z(k))))
    mixture = v.d3snd[z]
    for _, copy in reversed(d3):
        copy.wait_recv()
    for k in range(1, 8):
        mixture += v.d3rcv[k]
    out_ref[...] = (own + mixture).astype(BF16)[:, :112]

    for copy in sent:
        copy.wait_send()


def shards(queries, latent_cache, block_ids, value_lift_weight, out_weight, residual, norm_gain, expert_ids,
           expert_weights, gate_weight, up_weight, down_weight):
    vmem, anywhere = pl.BlockSpec(memory_space=pltpu.VMEM), pl.BlockSpec(memory_space=pl.ANY)
    scratch = [pltpu.VMEM(shape, dtype) for _, shape, dtype in BUFFERS]
    scratch.append(pltpu.SemaphoreType.DMA((27,)))
    for _, count in PAIRS:
        scratch += [pltpu.SemaphoreType.DMA((count,)), pltpu.SemaphoreType.DMA((count,))]
    return pl.pallas_call(
        kernel,
        out_shape=jax.ShapeDtypeStruct((8, 112), BF16),
        in_specs=[anywhere] * 12,
        out_specs=vmem,
        scratch_shapes=scratch,
        compiler_params=pltpu.CompilerParams(
            collective_id=0, has_side_effects=True, vmem_limit_bytes=56 * 1024 * 1024
        ),
        name="layer",
    )(
        block_ids, norm_gain.reshape(56, 128), expert_ids.T, expert_weights.T, residual,
        jnp.swapaxes(queries, 1, 2), jnp.swapaxes(latent_cache, 1, 2),
        value_lift_weight, out_weight, gate_weight, up_weight, down_weight,
    )


def solution(mesh):
    placed = (
        P("node", None, None),
        P("node", ("ctx", "dev"), None),
        P("node", None),
        P(("ctx", "dev"), None, None),
        P(("ctx", "dev"), None),
        P("node", None),
        P(),
        P(),
        P(),
        P(("node", "dev"), None, "ctx"),
        P(("node", "dev"), None, "ctx"),
        P(("node", "dev"), "ctx", None),
    )
    return jax.shard_map(
        shards, mesh=mesh, in_specs=placed, out_specs=P("node", ("ctx", "dev")), check_vma=False
    )
```

```python
import math

import jax
import jax.numpy as jnp
from jax import lax
from jax.experimental import pallas as pl
from jax.experimental.pallas import tpu as pltpu
from jax.sharding import PartitionSpec as P

MESH = pl.DeviceIdType.MESH
F32, BF16 = jnp.float32, jnp.bfloat16
score_scale = 192.0 ** (-0.5) * (0.1 * math.log(40.0) + 1.0) ** 2
floor_score = -1e30
norm_eps = 1e-06

PAIRS = (
    ("a1", 8), ("s1", 8), ("s2", 8), ("a2", 8), ("a3", 8), ("e1", 8), ("e2", 4), ("b1", 8),
    ("b2", 8), ("c1", 16), ("c2", 4), ("wd", 1), ("hid", 1), ("d2", 16), ("d3", 8),
)
BUFFERS = (
    ("ids", (8, 32), jnp.int32), ("gain_in", (56, 128), BF16), ("eid", (8, 32), jnp.int32), ("ew", (8, 32), F32),
    ("res", (8, 7168), BF16), ("qv", (8, 576, 128), BF16), ("cv", (8, 576, 256), BF16), ("liftv", (2, 512, 128), BF16),
    ("wov", (256, 7168), BF16), ("wguv", (7168, 256), BF16), ("wdv", (128, 7168), BF16),
    ("keep", (8, 256), F32), ("probs", (8, 128, 256), BF16),
    ("st1", (8, 16, 128), F32), ("st2", (8, 24, 128), F32), ("fcol", (128, 128), F32),
    ("a1own", (8, 64, 512), F32), ("a1snd", (8, 64, 512), BF16), ("a1rcv", (8, 64, 512), BF16),
    ("a2snd", (4, 6, 16, 512), BF16), ("a2rcv", (4, 6, 16, 512), BF16),
    ("e1snd", (8, 16, 512), BF16), ("e1rcv", (8, 16, 512), BF16), ("e2snd", (4, 16, 512), BF16), ("e2rcv", (4, 16, 512), BF16),
    ("a3snd", (8, 16, 512), BF16), ("a3rcv", (8, 16, 512), BF16),
    ("b1snd", (8, 16, 512), BF16), ("b1rcv", (8, 16, 512), BF16), ("part", (8, 16, 512), BF16),
    ("state", (32, 16, 512), BF16), ("normed", (4, 64, 512), BF16), ("gain", (8, 16, 512), F32),
    ("select", (4, 384, 256), BF16), ("laid", (2, 128, 4096), BF16), ("down", (256, 4096), BF16),
    ("hidden", (2, 32, 128), BF16), ("d2snd", (16, 4, 16, 128), BF16), ("d2rcv", (16, 4, 16, 128), BF16),
    ("d3snd", (8, 8, 128), F32), ("d3rcv", (8, 8, 128), F32),
)


ROWS_AT_ONCE = 4
SENT_AT_ONCE = 4
BLOCKS_AT_ONCE = 4


class Names:
    pass


def dot(a, b, dims=((1,), (0,))):
    return lax.dot_general(a, b, (dims, ((), ())), preferred_element_type=F32)


def iota(shape, dim):
    return lax.broadcasted_iota(jnp.int32, shape, dim)


def kernel(ids_hbm, gain_hbm, eid_hbm, ew_hbm, res_hbm, q_hbm, c_hbm, lift_hbm, wo_hbm, wg_hbm, wu_hbm, wd_hbm,
           out_ref, *scratch):
    v = Names()
    for (name, _, _), ref in zip(BUFFERS, scratch):
        setattr(v, name, ref)
    rest = scratch[len(BUFFERS):]
    local = rest[0]
    sems = {name: (rest[1 + 2 * i], rest[2 + 2 * i]) for i, (name, _) in enumerate(PAIRS)}

    ctx, node, dev = lax.axis_index("ctx"), lax.axis_index("node"), lax.axis_index("dev")
    z, core = lax.div(ctx, 2), lax.rem(ctx, 2)
    other = 1 - core
    g = core * 4 + dev
    shard = ctx * 4 + dev
    expert = node * 4 + dev

    def turn(a, k, n):
        return lax.rem(a + k, n)

    def at(ctx=ctx, node=node, dev=dev):
        return {"ctx": ctx, "node": node, "dev": dev}

    def at_core():
        return at(ctx=z * 2 + other)

    def at_z(k):
        return at(ctx=turn(z, k, 8) * 2 + core)

    def at_g(k):
        there = turn(g, k, 8)
        return at(ctx=z * 2 + lax.div(there, 4), dev=lax.rem(there, 4))

    def remote(name, slot, src, dst, where):
        send, recv = sems[name]
        return pltpu.make_async_remote_copy(
            src_ref=src, dst_ref=dst, send_sem=send.at[slot], recv_sem=recv.at[slot],
            device_id=where, device_id_type=MESH,
        )

    sent, fetches = [], []

    def push(*args):
        copy = remote(*args)
        copy.start()
        sent.append(copy)
        return copy

    def settle(flying):
        done = len(sent) - flying
        for copy in sent[:done]:
            copy.wait_send()
        del sent[:done]

    far_z, far_g = (4, 3, 5, 2, 6, 1, 7), (2, 6, 1, 3, 5, 7, 4)

    def hops(i, j):
        return min(i, 4 - i) + min(j, 4 - j)

    far_xy = sorted(((i, j) for i in range(4) for j in range(4) if i + j), key=lambda step: -hops(*step))

    barrier = pltpu.get_barrier_semaphore()
    partners = [(min(k, 8 - k), at_z(k)) for k in far_z]
    partners += [(2 if k in (2, 6) else k % 2, at_g(k)) for k in far_g]
    partners += [(hops(i, j), at(node=turn(node, i, 4), dev=turn(dev, j, 4))) for i in range(1, 4) for j in range(4)]
    for _, where in sorted(partners, key=lambda partner: -partner[0]):
        pl.semaphore_signal(barrier, inc=1, device_id=where, device_id_type=MESH)

    def fetch_q(r):
        return pltpu.make_async_copy(q_hbm.at[r], v.qv.at[r], local.at[r])

    def fetch_c(r):
        return pltpu.make_async_copy(c_hbm.at[r], v.cv.at[r], local.at[8 + r])

    fetch_ids = pltpu.make_async_copy(ids_hbm, v.ids, local.at[22])
    fetch_ids.start()
    for i in range(8):
        fetch_q(i).start()
        fetch_c(i).start()
    fetch_gain = pltpu.make_async_copy(gain_hbm, v.gain_in, local.at[23])
    fetch_eid = pltpu.make_async_copy(eid_hbm, v.eid, local.at[24])
    fetch_ew = pltpu.make_async_copy(ew_hbm, v.ew, local.at[25])
    fetch_res = pltpu.make_async_copy(res_hbm, v.res, local.at[26])
    fetch_lift = pltpu.make_async_copy(lift_hbm, v.liftv, local.at[16])
    fetch_wo = pltpu.make_async_copy(wo_hbm, v.wov, local.at[17])
    fetch_wg = pltpu.make_async_copy(wg_hbm.at[0], v.wguv.at[:, pl.ds(0, 128)], local.at[18])
    fetch_wu = pltpu.make_async_copy(wu_hbm.at[0], v.wguv.at[:, pl.ds(128, 128)], local.at[19])
    fetch_wd = pltpu.make_async_copy(wd_hbm.at[0], v.wdv, local.at[20])
    for copy in (fetch_gain, fetch_eid, fetch_ew, fetch_res, fetch_wd, fetch_lift, fetch_wo, fetch_wg, fetch_wu):
        copy.start()
        fetches.append(copy)

    def ready(*copies):
        for copy in copies:
            fetches[:] = [other_copy for other_copy in fetches if other_copy is not copy]
            copy.wait()

    fetch_ids.wait()
    ids = v.ids[...]
    block = lax.div(iota((8, 256), 1), 64)
    keep = jnp.zeros((8, 256), F32)
    for b in range(4):
        hit = jnp.max(jnp.where(ids == shard * 4 + b, 1.0, 0.0), axis=1, keepdims=True)
        keep = jnp.where(block == b, hit, keep)
    v.keep[...] = keep

    def one_hot(hit):
        return jnp.where(hit, 1.0, 0.0).astype(BF16)

    at_row, at_col = iota((128, 128), 0), iota((128, 128), 1)

    def part_of(number, low, size):
        return lax.rem(lax.div(number, low), size)

    by_owner = one_hot(
        at_col == part_of(at_row, 2, 8) * 16 + part_of(at_row, 64, 2) * 8 + part_of(at_row, 16, 4) * 2 + part_of(at_row, 1, 2)
    )
    stats = jnp.zeros((128, 128), F32)
    for r in range(8):
        if r % ROWS_AT_ONCE == 0:
            for i in range(r, r + ROWS_AT_ONCE):
                fetch_q(i).wait()
                fetch_c(i).wait()
        kept = v.keep[r:r + 1, :] > 0.5
        heads = dot(by_owner, v.qv[r], ((1,), (1,))).astype(BF16)
        scores = dot(heads, v.cv[r]) * score_scale
        scores = jnp.where(kept, scores, floor_score)
        top = jnp.max(scores, axis=1, keepdims=True)
        probs = jnp.where(kept, jnp.exp(scores - top), 0.0).astype(BF16)
        total = jnp.sum(probs.astype(F32), axis=1, keepdims=True)
        v.probs[r] = probs
        stats = jnp.where(at_col == r, top, jnp.where(at_col == r + 8, total, stats))
    stats = stats.T[:16, :]

    v.st1[g] = stats
    pl.semaphore_wait(barrier, len(partners))
    s1 = {k: push("s1", k, v.st1.at[g], v.st1.at[g], at_g(k)) for k in (4,) + far_g[:6]}

    a1 = []
    for r in range(8):
        num = dot(v.probs[r], v.cv[r, :512, :], ((1,), (1,)))
        v.a1snd[r] = jnp.where(core == 0, num[64:], num[:64]).astype(BF16)
        v.a1own[r] = jnp.where(core == 0, num[:64], num[64:])
        if r % SENT_AT_ONCE == SENT_AT_ONCE - 1:
            for i in range(r + 1 - SENT_AT_ONCE, r + 1):
                a1.append(push("a1", i, v.a1snd.at[i], v.a1rcv.at[i], at_core()))

    def joined(ref):
        peak = ref[0, :8, :]
        for i in range(1, 8):
            peak = jnp.maximum(peak, ref[i, :8, :])
        total = jnp.zeros((8, 128), F32)
        for i in range(8):
            total += ref[i, 8:16, :] * jnp.exp(ref[i, :8, :] - peak)
        return peak, total

    def pair_top(x):
        return jnp.maximum(v.st1[x, :8, :], v.st1[4 + x, :8, :])

    s1.pop(4).wait_recv()
    pair = pair_top(dev)
    here = jnp.exp(v.st1[g, :8, :] - pair)
    there = jnp.exp(v.st1[other * 4 + dev, :8, :] - pair)
    v.fcol[...] = jnp.concatenate([here, there, jnp.zeros((112, 128), F32)], axis=0).T

    half = pl.ds(pl.multiple_of(core * 64, 64), 64)

    def core_join(r):
        both = v.fcol[half, r:r + 1] * v.a1own[r] + v.fcol[half, r + 8:r + 9] * v.a1rcv[r].astype(F32)
        return both.astype(BF16)

    a2 = []
    for c in range(2):
        for copy in a1[3 * c:3 * c + 3]:
            copy.wait_recv()
        for r in range(3 * c, 3 * c + 3):
            both = core_join(r)
            for x in range(4):
                v.a2snd[x, r] = both[x * 16:x * 16 + 16]
        chunk = pl.ds(3 * c, 3)
        for k in (2, 1, 3):
            xt = turn(dev, k, 4)
            a2.append(push("a2", k + c * 4, v.a2snd.at[xt, chunk], v.a2rcv.at[k, chunk], at(dev=xt)))
    for copy in a1[6:]:
        copy.wait_recv()
    to_z = one_hot(
        at_col == part_of(at_row, 1, 2) * 64 + part_of(at_row, 4, 4) * 16 + part_of(at_row, 16, 8) * 2 + part_of(at_row, 2, 2)
    )
    late = dot(to_z, jnp.concatenate([core_join(6), core_join(7)], axis=0))
    v.e1snd[...] = late.astype(BF16).reshape(8, 16, 512)
    e1 = [push("e1", k, v.e1snd.at[turn(z, k, 8)], v.e1rcv.at[k], at_z(k)) for k in far_z]
    ready(fetch_gain)
    for i in range(8):
        for t in range(4):
            row = i * 7 + t
            v.gain[i, :8, t * 128:t * 128 + 128] = jnp.broadcast_to(v.gain_in[row:row + 1, :].astype(F32), (8, 128))
            v.gain[i, 8:, t * 128:t * 128 + 128] = jnp.broadcast_to(v.gain_in[row + 3:row + 4, :].astype(F32), (8, 128))

    spans = ((0, 256), (128, 384), (384, 384), (640, 256))
    into, outof = iota((384, 256), 1), iota((384, 256), 0)
    for i, (first, _) in enumerate(spans):
        source = i * 224 - first + lax.div(into, 128) * 112 + lax.rem(into, 128)
        v.select[i] = one_hot((outof == source) & (lax.rem(into, 128) < 112))

    def lay_out(blocks):
        for zt in blocks:
            for i, (first, width) in enumerate(spans):
                columns = v.wdv[:, zt * 896 + first:zt * 896 + first + width]
                piece = dot(columns, v.select[i, :width, :]).astype(BF16)
                v.laid[i // 2, :, zt * 512 + i % 2 * 256:zt * 512 + i % 2 * 256 + 256] = piece

    for copy in s1.values():
        copy.wait_recv()
    peak, total = joined(v.st1)
    v.st2[z, :8, :] = peak
    v.st2[z, 8:16, :] = total
    v.st2[z, 16:, :] = pair
    s2 = [push("s2", k, v.st2.at[z], v.st2.at[z], at_z(k)) for k in far_z]

    factors = [jnp.exp(pair_top(turn(dev, 4 - k, 4)) - peak) for k in range(4)]
    v.fcol[...] = jnp.concatenate(factors + [jnp.zeros((96, 128), F32)], axis=0).T
    ready(fetch_wd)
    lay_out(range(2))

    sixteen = pl.ds(pl.multiple_of(core * 64 + dev * 16, 16), 16)
    by_row, by_col = iota((128, 48), 0), iota((128, 48), 1)
    latents = jnp.zeros((128, 512), F32)
    for c in range(2):
        for copy in a2[3 * c:3 * c + 3]:
            copy.wait_recv()
        rows = []
        for r in range(3 * c, 3 * c + 3):
            row = v.fcol[sixteen, r:r + 1] * v.a2snd[dev, r].astype(F32)
            for k in range(1, 4):
                row += v.fcol[sixteen, k * 8 + r:k * 8 + r + 1] * v.a2rcv[k, r].astype(F32)
            rows.append(row.astype(BF16))
        by_z = one_hot(by_col + c * 48 == part_of(by_row, 1, 8) * 16 + part_of(by_row, 16, 8) * 2 + part_of(by_row, 8, 2))
        latents += dot(by_z, jnp.concatenate(rows, axis=0))

    v.a3snd[...] = latents.astype(BF16).reshape(8, 16, 512)
    a3 = []
    for k in far_z:
        zt = turn(z, k, 8)
        a3.append((k, push("a3", k, v.a3snd.at[zt], v.a3rcv.at[k], at_z(k))))
    for copy in s2:
        copy.wait_recv()
    peak, total = joined(v.st2)

    late_row, late_lane = iota((16, 128), 0), iota((16, 128), 1)
    late_head = late_lane == core * 64 + part_of(late_row, 4, 4) * 16 + z * 2 + part_of(late_row, 2, 2)

    def late_factor(zt):
        factor = jnp.exp(v.st2[zt, 16:, :] - peak) / total
        factor = jnp.where(part_of(late_row, 1, 2) == 0, factor[6:7], factor[7:8])
        return jnp.sum(jnp.where(late_head, factor, 0.0), axis=1, keepdims=True)

    late_factors = [late_factor(turn(z, 8 - k, 8)) for k in range(8)]
    for copy in reversed(e1):
        copy.wait_recv()
    late = late_factors[0] * v.e1snd[z].astype(F32)
    for k in range(1, 8):
        late += late_factors[k] * v.e1rcv[k].astype(F32)
    to_row, to_col = iota((64, 16), 0), iota((64, 16), 1)
    to_x = one_hot(
        (part_of(to_row, 1, 8) >= 6)
        & (to_col == part_of(to_row, 16, 4) * 4 + part_of(to_row, 8, 2) * 2 + part_of(to_row, 1, 8) - 6)
    )
    v.e2snd[...] = dot(to_x, late.astype(BF16)).astype(BF16).reshape(4, 16, 512)
    e2 = [push("e2", k, v.e2snd.at[turn(dev, k, 4)], v.e2rcv.at[k], at(dev=turn(dev, k, 4))) for k in (2, 1, 3)]
    lay_out(range(2, 5))
    ready(fetch_lift, fetch_wo)

    own_lane = iota((8, 128), 1) - (core * 64 + dev * 16 + z * 2)

    def factor_of(zt):
        factor = jnp.exp(v.st2[zt, :8, :] - peak) / total
        columns = [jnp.sum(jnp.where(own_lane == h, factor, 0.0), axis=1, keepdims=True) for h in range(2)]
        return jnp.concatenate(columns, axis=0)

    factors = [factor_of(turn(z, 8 - k, 8)) for k in range(8)]
    summed = factors[0] * v.a3snd[z].astype(F32)
    for _, copy in reversed(a3):
        copy.wait_recv()
    for k in range(1, 8):
        summed += factors[k] * v.a3rcv[k].astype(F32)
    for copy in e2:
        copy.wait_recv()
    summed += v.e2snd[dev].astype(F32)
    for k in range(1, 4):
        summed += v.e2rcv[k].astype(F32)
    own_heads = summed.astype(BF16)
    values = jnp.concatenate([dot(own_heads, v.liftv[0])[:8], dot(own_heads, v.liftv[1])[8:]], axis=1).astype(BF16)

    def projected(i):
        upper = dot(values, v.wov[:, pl.ds(pl.multiple_of(i * 896, 128), 512)])
        lower = dot(values, v.wov[:, pl.ds(pl.multiple_of(i * 896 + 512, 128), 384)])
        return jnp.concatenate([upper, jnp.concatenate([upper[:, 384:], lower], axis=1)], axis=0)

    b1 = []
    for i in range(0, 7, BLOCKS_AT_ONCE):
        for k in far_g[i:i + BLOCKS_AT_ONCE]:
            gt = turn(g, k, 8)
            v.b1snd[gt] = projected(gt).astype(BF16)
        for k in far_g[i:i + BLOCKS_AT_ONCE]:
            b1.append((k, push("b1", k, v.b1snd.at[turn(g, k, 8)], v.b1rcv.at[k], at_g(k))))
    summed = projected(g)
    ready(fetch_res)
    residual = jnp.concatenate(
        [
            v.res[:, pl.ds(pl.multiple_of(g * 896, 128), 512)].astype(F32),
            v.res[:, pl.ds(pl.multiple_of(g * 896 + 384, 128), 512)].astype(F32),
        ],
        axis=0,
    )
    for _, copy in reversed(b1):
        copy.wait_recv()
    for k in range(1, 8):
        summed += v.b1rcv[k].astype(F32)
    v.part[z] = summed.astype(BF16)
    b2 = [push("b2", k, v.part.at[z], v.part.at[z], at_z(k)) for k in far_z]
    lay_out(range(5, 8))
    mine_rows = pl.ds(pl.multiple_of(core * 128, 128), 128)
    wd = push("wd", 0, v.laid.at[other], v.down.at[mine_rows], at_core())
    keep_wd = pltpu.make_async_copy(v.laid.at[core], v.down.at[mine_rows], local.at[21])
    keep_wd.start()
    fetches.append(keep_wd)
    settle(8)
    ready(fetch_wg, fetch_wu)
    for copy in b2:
        copy.wait_recv()
    attention = v.part[0].astype(F32)
    for i in range(1, 8):
        attention += v.part[i].astype(F32)
    mine = core * 16 + node * 4 + dev
    v.state[mine] = (residual + attention).astype(BF16)

    c1, c2 = {}, []
    for i, j in far_xy:
        where = at(node=turn(node, i, 4), dev=turn(dev, j, 4))
        c1[i, j] = push("c1", i * 4 + j, v.state.at[mine], v.state.at[mine], where)
    ready(fetch_eid, fetch_ew)
    coef = jnp.sum(jnp.where(v.eid[...] == expert, v.ew[...], 0.0), axis=0, keepdims=True)
    coef = jnp.sum(jnp.where(iota((32, 32), 0) == iota((32, 32), 1), coef, 0.0), axis=1, keepdims=True)
    settle(16)
    for i in (0, 1, 3, 2):
        for j in range(4):
            if i + j > 0:
                c1[i, j].wait_recv()
        came = pl.ds(core * 16 + turn(node, 4 - i, 4) * 4, 4)
        c2.append(push("c2", i, v.state.at[came], v.state.at[came], at_core()))

    squares = [jnp.zeros((16, 512), F32) for _ in range(4)]
    upper = jnp.zeros((64, 256), F32)
    lower = jnp.zeros((64, 256), F32)
    for c in (core, other):
        for i in range(4):
            block = c * 4 + i
            for y in range(4):
                wide = v.state[c * 16 + y * 4 + i].astype(F32)
                squares[y] += wide * wide
                v.normed[i, y * 16:y * 16 + 16, :] = (wide * v.gain[block]).astype(BF16)
            first = pl.multiple_of(block * 896, 128)
            upper += dot(v.normed[i], v.wguv[pl.ds(first, 512), :])
            lower += dot(v.normed[i, :, 128:], v.wguv[pl.ds(first + 512, 384), :])
        if c is core:
            for copy in c2:
                copy.wait_recv()
    once = (iota((16, 512), 0) < 8) | (iota((16, 512), 1) >= 128)
    scale = []
    for y in range(4):
        square = jnp.sum(jnp.where(once, squares[y], 0.0), axis=1, keepdims=True)
        scale.append(lax.rsqrt((square[:8] + square[8:]) / 7168.0 + norm_eps))
    both = jnp.concatenate([upper[y * 16:y * 16 + 8] + lower[y * 16 + 8:y * 16 + 16] for y in range(4)], axis=0)
    both = both * jnp.concatenate(scale, axis=0)
    gate, up = both[:, :128], both[:, 128:]
    v.hidden[core] = (gate / (1.0 + jnp.exp(-gate)) * up * coef).astype(BF16)
    hid = push("hid", 0, v.hidden.at[core], v.hidden.at[core], at_core())

    own = v.state[lax.div(z, 4) * 16 + node * 4 + lax.rem(z, 4)]
    own = dot(own, one_hot(iota((512, 128), 0) == iota((512, 128), 1) + core * 64 + dev * 112))
    own = jnp.where(core == 0, own[:8], own[8:])

    ready(keep_wd)
    wd.wait_recv()
    hid.wait_recv()
    hidden = jnp.concatenate([v.hidden[0], v.hidden[1]], axis=1)
    for i in range(4):
        first = dot(hidden, v.down[:, i * 1024:i * 1024 + 512])
        second = dot(hidden, v.down[:, i * 1024 + 512:i * 1024 + 1024])
        for y in range(4):
            pair = jnp.concatenate([first[y * 8:y * 8 + 8], second[y * 8:y * 8 + 8]], axis=0).astype(BF16)
            for x in range(4):
                v.d2snd[y * 4 + x, i] = pair[:, x * 128:x * 128 + 128]
    d2 = []
    for i, j in far_xy:
        yt, xt = turn(node, i, 4), turn(dev, j, 4)
        d2.append((i * 4 + j, push("d2", i * 4 + j, v.d2snd.at[yt * 4 + xt], v.d2rcv.at[i * 4 + j], at(node=yt, dev=xt))))
    settle(15)
    mixture = [v.d2snd[node * 4 + dev, i].astype(F32) for i in range(4)]
    for _, copy in reversed(d2):
        copy.wait_recv()
    for k in range(1, 16):
        for i in range(4):
            mixture[i] += v.d2rcv[k, i].astype(F32)
    for i in range(4):
        v.d3snd[2 * i] = mixture[i][:8]
        v.d3snd[2 * i + 1] = mixture[i][8:]
    d3 = []
    for k in far_z:
        d3.append((k, push("d3", k, v.d3snd.at[turn(z, k, 8)], v.d3rcv.at[k], at_z(k))))
    settle(7)
    mixture = v.d3snd[z]
    for _, copy in reversed(d3):
        copy.wait_recv()
    for k in range(1, 8):
        mixture += v.d3rcv[k]
    out_ref[...] = (own + mixture).astype(BF16)[:, :112]

    for copy in sent:
        copy.wait_send()


def shards(queries, latent_cache, block_ids, value_lift_weight, out_weight, residual, norm_gain, expert_ids,
           expert_weights, gate_weight, up_weight, down_weight):
    vmem, anywhere = pl.BlockSpec(memory_space=pltpu.VMEM), pl.BlockSpec(memory_space=pl.ANY)
    scratch = [pltpu.VMEM(shape, dtype) for _, shape, dtype in BUFFERS]
    scratch.append(pltpu.SemaphoreType.DMA((27,)))
    for _, count in PAIRS:
        scratch += [pltpu.SemaphoreType.DMA((count,)), pltpu.SemaphoreType.DMA((count,))]
    return pl.pallas_call(
        kernel,
        out_shape=jax.ShapeDtypeStruct((8, 112), BF16),
        in_specs=[anywhere] * 12,
        out_specs=vmem,
        scratch_shapes=scratch,
        compiler_params=pltpu.CompilerParams(
            collective_id=0, has_side_effects=True, vmem_limit_bytes=56 * 1024 * 1024
        ),
        name="layer",
    )(
        block_ids, norm_gain.reshape(56, 128), expert_ids.T, expert_weights.T, residual,
        jnp.swapaxes(queries, 1, 2), jnp.swapaxes(latent_cache, 1, 2),
        value_lift_weight, out_weight, gate_weight, up_weight, down_weight,
    )


def solution(mesh):
    placed = (
        P("node", None, None),
        P("node", ("ctx", "dev"), None),
        P("node", None),
        P(("ctx", "dev"), None, None),
        P(("ctx", "dev"), None),
        P("node", None),
        P(),
        P(),
        P(),
        P(("node", "dev"), None, "ctx"),
        P(("node", "dev"), None, "ctx"),
        P(("node", "dev"), "ctx", None),
    )
    return jax.shard_map(
        shards, mesh=mesh, in_specs=placed, out_specs=P("node", ("ctx", "dev")), check_vma=False
    )
```
